768 devices in a mesh: yy: 2 (over core), lat: 24 (over x_lo, z), lon: 16 (over x_hi, y).
Axes of the slice: x: 4 (x_hi: 2, x_lo: 2; x = x_hi * 2 + x_lo), y: 8, z: 12, core: 2. Of those that a mesh axis runs over, the one named last changes fastest.
Arguments:
- fields_in: float32 [2, 5, 384, 36864], P('yy', None, 'lat', 'lon'), may hold values from -6 to 6
- viscosity: float32 [2, 384, 36864], P('yy', 'lat', 'lon'), may hold values from 0.02 to 0.4
- lat_weights: float32 [2, 24, 16, 18, 128], P('yy', 'lat', 'lon'), may hold values from -0.5 to 0.5
- lon_weights: float32 [2, 24, 16, 6, 128], P('yy', 'lat', 'lon'), may hold values from -0.5 to 0.5
- lat_angles: float32 [2, 24, 16, 18], P('yy', 'lat', 'lon'), may hold values from -3.140625 to 3.140625
- lon_angles: float32 [2, 24, 16, 6], P('yy', 'lat', 'lon'), may hold values from -3.140625 to 3.140625
- patch_rows: int32 [2, 24, 16, 2], P('yy', 'lat', 'lon'), may hold values from 0 to 8
- patch_cols: int32 [2, 24, 16, 2], P('yy', 'lat', 'lon'), may hold values from 0 to 56
- lat_pairing: int32 [2, 16, 24], P(None, 'lon'), may hold values from 0 to 23, each once within a row
- lon_pairing: int32 [2, 24, 16], P(None, 'lat'), may hold values from 0 to 15, each once within a row
Outputs:
- fields_out: float32 [2, 5, 384, 36864], P('yy', None, 'lat', 'lon')
The draws below stay inside these ranges and needn't reach their ends.
Inputs may be any that keep to these rules, and one draw needn't show every extreme that they name: `lat_pairing`: for every receiving panel and longitude tile, the entries over the 24 source tiles are each block number once. `lon_pairing`: for every receiving panel and latitude tile, the entries over the 16 source tiles are each block number once.
All inputs are finite; a program needn't handle non-finite values.
Results may differ from the reference program's by a relative error of at most 0.0003.
Values sent between devices are 32-bit elements; how exact they have to be, the bound alone decides.
A program may use at most 32 MiB of HBM per device.

```python
import math
import jax
import jax.numpy as jnp
from jax import lax

FIELDS = 5
CLAT = 16
CLON = 72
LEV = 32
PATCH_H = 8
PATCH_W = 16
NLAT = 384
NLON = 1152
LAT_BLOCK = 18
LON_BLOCK = 6
N_LAT = 24
N_LON = 16


def plant(entries, own_key, low, high):
    shape = entries.shape
    place = [jax.random.randint(jax.random.fold_in(own_key, axis), (), 0, shape[axis]) for axis in range(len(shape))]
    entries = entries.at[tuple(place)].set(low)
    longest = shape.index(max(shape))
    place[longest] = (place[longest] + 1) % shape[longest]
    return entries.at[tuple(place)].set(high)


def block_levels(key, dims, split, low, largest):
    level = 1.0
    for axis_at, blocks in split:
        steps = jax.random.uniform(jax.random.fold_in(jax.random.fold_in(key, 6), axis_at), (blocks,), jnp.float32, low / len(split), largest / len(split))
        level = level * jnp.repeat(jnp.exp(steps), dims[axis_at] // blocks).reshape((-1,) + (1,) * (len(dims) - 1 - axis_at))
    return level


def bell_draw(stream_key, extent, deviation, bound, pieces=(), kind=jnp.bfloat16):
    level = block_levels(stream_key, extent, pieces, -0.22, 0.18) if pieces else 1.0
    values = jax.random.normal(stream_key, extent, jnp.float32) * deviation * level
    return jnp.minimum(jnp.maximum(values, -bound), bound).astype(kind)


def setup_inputs(seed: int = 0) -> dict:
    streams_of = jax.random.split(jax.random.key(seed), 11)
    fields_in = bell_draw(streams_of[0], (2, FIELDS, NLAT, NLON * LEV), 1.0, 6.0, ((0, 2), (2, 24), (3, 16)), jnp.float32)
    viscosity = jnp.clip(jnp.exp(math.log(0.4) - 2.9957323 * jax.random.uniform(streams_of[1], (2, NLAT, NLON * LEV), jnp.float32) ** block_levels(streams_of[1], (2, NLAT, NLON * LEV), ((0, 2), (1, 24), (2, 16)), -0.2, 0.2)), 0.02, 0.4)
    lat_weights = bell_draw(streams_of[2], (2, N_LAT, N_LON, LAT_BLOCK, PATCH_H * PATCH_W), (PATCH_H * PATCH_W) ** -0.5, 0.5, ((0, 2), (1, 24), (2, 16)), jnp.float32)
    lon_weights = bell_draw(streams_of[3], (2, N_LAT, N_LON, LON_BLOCK, PATCH_H * PATCH_W), (PATCH_H * PATCH_W) ** -0.5, 0.5, ((0, 2), (1, 24), (2, 16)), jnp.float32)
    lat_angles = jnp.clip(jax.random.uniform(streams_of[4], (2, N_LAT, N_LON, LAT_BLOCK), jnp.float32, -3.140625, 3.140625), -3.140625, 3.140625)
    lon_angles = jnp.clip(jax.random.uniform(streams_of[5], (2, N_LAT, N_LON, LON_BLOCK), jnp.float32, -3.140625, 3.140625), -3.140625, 3.140625)
    patch_rows = plant(jax.random.randint(streams_of[6], (2, N_LAT, N_LON, 2), 0, CLAT - PATCH_H + 1), jax.random.fold_in(streams_of[6], 1), 0, CLAT - PATCH_H).astype(jnp.int32)
    patch_cols = plant(jax.random.randint(streams_of[7], (2, N_LAT, N_LON, 2), 0, CLON - PATCH_W + 1), jax.random.fold_in(streams_of[7], 1), 0, CLON - PATCH_W).astype(jnp.int32)
    lat_pairing = jax.vmap(lambda own: jax.random.permutation(own, N_LAT))(jax.random.split(streams_of[8], 2 * N_LON)).reshape((2, N_LON, N_LAT)).astype(jnp.int32)
    lon_pairing = jax.vmap(lambda own: jax.random.permutation(own, N_LON))(jax.random.split(streams_of[9], 2 * N_LAT)).reshape((2, N_LAT, N_LON)).astype(jnp.int32)
    return dict(fields_in=fields_in, viscosity=viscosity, lat_weights=lat_weights, lon_weights=lon_weights, lat_angles=lat_angles, lon_angles=lon_angles, patch_rows=patch_rows, patch_cols=patch_cols, lat_pairing=lat_pairing, lon_pairing=lon_pairing)


TIME_STEP = 0.2
KAPPA_PRESS = 0.4
GAMMA_HEAT = 1.4


def row_shift(padded, offset):
    height = padded.shape[1] - 6
    width = padded.shape[2] - 6
    return padded[:, 3 + offset:3 + offset + height, 3:3 + width, :]


def col_shift(padded, offset):
    height = padded.shape[1] - 6
    width = padded.shape[2] - 6
    return padded[:, 3:3 + height, 3 + offset:3 + offset + width, :]


def sixth_order(padded, shifter):
    return (45.0 * (shifter(padded, 1) - shifter(padded, -1)) - 9.0 * (shifter(padded, 2) - shifter(padded, -2)) + (shifter(padded, 3) - shifter(padded, -3))) / 60.0


def vertical(interior):
    widened = jnp.pad(interior, ((0, 0), (0, 0), (0, 0), (1, 1)))
    return 0.5 * (widened[..., 2:] - widened[..., :-2])


def latitude_cosine(first_row, count, total_rows):
    rows_float = (first_row + jnp.arange(count, dtype=jnp.int32)).astype(jnp.float32)
    return jnp.cos((rows_float + 0.5 - 0.5 * total_rows) * (0.5 * math.pi / total_rows))


def tendency(padded, cell_visc, cosine):
    interior = row_shift(padded, 0)
    metric = cosine[None, :, None, None]
    along_lat = sixth_order(padded, row_shift)
    along_lon = sixth_order(padded, col_shift) / metric
    along_lev = vertical(interior)
    laplace = row_shift(padded, 1) + row_shift(padded, -1) - 2.0 * interior + (col_shift(padded, 1) + col_shift(padded, -1) - 2.0 * interior) / (metric * metric)
    advection = interior[1:2] * along_lon + interior[2:3] * along_lat + interior[3:4] * along_lev
    divergence = along_lon[1] + along_lat[2] + along_lev[3]
    forcing = jnp.stack([-divergence, -KAPPA_PRESS * along_lon[4], -KAPPA_PRESS * along_lat[4], -KAPPA_PRESS * along_lev[4] - interior[0], -GAMMA_HEAT * divergence])
    return forcing - advection + cell_visc[None] * laplace


def rim_export(tile_fields, row_start, col_start, matrix, angles):
    zero_index = jnp.zeros((), jnp.int32)
    source_patch = lax.dynamic_slice(tile_fields, (zero_index, row_start.astype(jnp.int32), col_start.astype(jnp.int32), zero_index), (tile_fields.shape[0], PATCH_H, PATCH_W, tile_fields.shape[3]))
    flat = source_patch.reshape(tile_fields.shape[0], PATCH_H * PATCH_W, tile_fields.shape[3])
    interp = jnp.einsum('ts,fsl->ftl', matrix, flat, precision=lax.Precision.HIGHEST)
    cos_angle = jnp.cos(angles)[:, None]
    sin_angle = jnp.sin(angles)[:, None]
    east_part = cos_angle * interp[1] + sin_angle * interp[2]
    north_part = -sin_angle * interp[1] + cos_angle * interp[2]
    return jnp.stack([interp[0], east_part, north_part, interp[3], interp[4]])


def panel_exports(panel_fields, rows_here, cols_here, matrices, angles):
    tiles = panel_fields.reshape(FIELDS, N_LAT, CLAT, N_LON, CLON, LEV).transpose(1, 3, 0, 2, 4, 5)
    return jax.vmap(jax.vmap(rim_export))(tiles, rows_here, cols_here, matrices, angles)


def full_tendency(current, viscosity, lat_weights, lon_weights, lat_angles, lon_angles, patch_rows, patch_cols, lat_pairing, lon_pairing):
    cosine = latitude_cosine(0, NLAT, NLAT)
    lat_out = []
    lon_out = []
    for panel in range(2):
        lat_out.append(panel_exports(current[panel], patch_rows[panel, :, :, 0], patch_cols[panel, :, :, 0], lat_weights[panel], lat_angles[panel]))
        lon_out.append(panel_exports(current[panel], patch_rows[panel, :, :, 1], patch_cols[panel, :, :, 1], lon_weights[panel], lon_angles[panel]))
    results = []
    lat_blocks = jnp.arange(N_LAT, dtype=jnp.int32)
    lon_blocks = jnp.arange(N_LON, dtype=jnp.int32)
    for panel in range(2):
        other = 1 - panel
        lat_select = (lat_pairing[panel][:, :, None] == lat_blocks[None, None, :]).astype(jnp.float32)
        lat_strips = jnp.einsum('bak,abftl->bfktl', lat_select, lat_out[other], precision=lax.Precision.HIGHEST)
        lat_strips = lat_strips.reshape(N_LON, FIELDS, 6, CLON, LEV)
        south = lat_strips[:, :, 0:3].transpose(1, 2, 0, 3, 4).reshape(FIELDS, 3, NLON, LEV)
        north = lat_strips[:, :, 3:6].transpose(1, 2, 0, 3, 4).reshape(FIELDS, 3, NLON, LEV)
        lon_select = (lon_pairing[panel][:, :, None] == lon_blocks[None, None, :]).astype(jnp.float32)
        lon_strips = jnp.einsum('abk,abftl->afktl', lon_select, lon_out[other], precision=lax.Precision.HIGHEST)
        lon_strips = lon_strips.reshape(N_LAT, FIELDS, CLAT, 6, LEV)
        west = lon_strips[:, :, :, 0:3].transpose(1, 0, 2, 3, 4).reshape(FIELDS, NLAT, 3, LEV)
        east = lon_strips[:, :, :, 3:6].transpose(1, 0, 2, 3, 4).reshape(FIELDS, NLAT, 3, LEV)
        padded = jnp.pad(current[panel], ((0, 0), (3, 3), (3, 3), (0, 0)))
        padded = padded.at[:, 0:3, 3:3 + NLON].set(south)
        padded = padded.at[:, NLAT + 3:NLAT + 6, 3:3 + NLON].set(north)
        padded = padded.at[:, 3:3 + NLAT, 0:3].set(west)
        padded = padded.at[:, 3:3 + NLAT, NLON + 3:NLON + 6].set(east)
        results.append(tendency(padded, viscosity[panel], cosine))
    return jnp.stack(results)


def reference(fields_in, viscosity, lat_weights, lon_weights, lat_angles, lon_angles, patch_rows, patch_cols, lat_pairing, lon_pairing):
    start = fields_in.reshape(2, FIELDS, NLAT, NLON, LEV)
    visc = viscosity.reshape(2, NLAT, NLON, LEV)
    extras = (visc, lat_weights, lon_weights, lat_angles, lon_angles, patch_rows, patch_cols, lat_pairing, lon_pairing)
    first_section = start + TIME_STEP * full_tendency(start, *extras)
    second_rate = full_tendency(first_section, *extras)
    result = 0.5 * (start + first_section + TIME_STEP * second_rate)
    return result.reshape(2, FIELDS, NLAT, NLON * LEV)
```

```python
import math

import jax
import jax.numpy as jnp
from jax import lax
from jax.experimental import pallas as pl
from jax.experimental.pallas import tpu as pltpu
from jax.sharding import PartitionSpec as P

FIELDS = 5
LEV = 32
CLAT = 16
GROUPS = 18
LANES = 128
PATCH_H = 8
PATCH_W = 16
LAT_BLOCK = 18
LON_BLOCK = 6
SPAN = 5
TOP = 8

TIME_STEP = 0.2
KAPPA_PRESS = 0.4
GAMMA_HEAT = 1.4

MESH = pl.DeviceIdType.MESH
HIGHEST = lax.Precision.HIGHEST


def dot(left, right):
    return jnp.dot(left, right, precision=HIGHEST, preferred_element_type=jnp.float32)


def iota(shape, axis):
    return lax.broadcasted_iota(jnp.int32, shape, axis)


def kernel(
    n_lat,
    n_lon,
    fields,
    visc,
    lat_w,
    lon_w,
    lat_ang,
    lon_ang,
    rows,
    cols,
    lat_pair,
    lon_pair,
    out,
    x1,
    x2,
    wp,
    mat,
    zbuf,
    wbuf,
    rl,
    rw,
    halo_send,
    halo_recv,
    rim_send,
    rim_recv,
):
    p = lax.axis_index("yy")
    a = lax.axis_index("lat")
    b = lax.axis_index("lon")
    q = 1 - p
    low_a, high_a = a == 0, a == n_lat - 1
    low_b, high_b = b == 0, b == n_lon - 1
    neighbours = (
        (jnp.logical_not(low_a), (p, a - 1, b)),
        (jnp.logical_not(high_a), (p, a + 1, b)),
        (jnp.logical_not(low_b), (p, a, b - 1)),
        (jnp.logical_not(high_b), (p, a, b + 1)),
    )

    barrier = pltpu.get_barrier_semaphore()
    for there, device in neighbours:

        @pl.when(there)
        def _():
            pl.semaphore_signal(barrier, inc=1, device_id=device, device_id_type=MESH)

    @pl.when(jnp.logical_or(low_a, high_a))
    def _():
        def one(i, carry):
            pl.semaphore_signal(barrier, inc=1, device_id=(q, i, b), device_id_type=MESH)
            return carry

        lax.fori_loop(0, n_lat, one, 0)

    @pl.when(jnp.logical_or(low_b, high_b))
    def _():
        def one(i, carry):
            pl.semaphore_signal(barrier, inc=1, device_id=(q, a, i), device_id_type=MESH)
            return carry

        lax.fori_loop(0, n_lon, one, 0)

    for f in range(FIELDS):
        for g in range(GROUPS):
            x1[f, g + 1, TOP : TOP + CLAT, :] = fields[0, f, :, g * LANES : (g + 1) * LANES]

    wp[...] = jnp.zeros_like(wp)
    for t in range(LAT_BLOCK):
        u, v = t // 4, t % 4
        wp[0, v * 8 + u : v * 8 + u + 1, :] = lat_w[0, 0, 0, t : t + 1, :]
    for t in range(LON_BLOCK):
        u, v = (5, t + 1) if t < 3 else (6, t - 3)
        wp[1, v * 8 + u : v * 8 + u + 1, :] = lon_w[0, 0, 0, t : t + 1, :]
    entry = iota((LANES, GROUPS * CLAT), 0)
    place = iota((LANES, GROUPS * CLAT), 1)
    entry_row, entry_col = entry >> 4, entry & (PATCH_W - 1)
    place_row, place_col = place & (CLAT - 1), 4 * (place >> 4)
    same_row, from_col = [], []
    for j in range(2):
        same_row.append(place_row - entry_row == rows[0, 0, 0, j])
        from_col.append(entry_col - place_col + cols[0, 0, 0, j])
    for kk in range(4):
        part = None
        for j in range(2):
            chosen = jnp.where(jnp.logical_and(same_row[j], from_col[j] == kk), 1.0, 0.0)
            term = dot(wp[j], chosen)
            part = term if part is None else part + term
        mat[kk * 32 : (kk + 1) * 32, :] = part

    lane = iota((8, LANES), 1)
    sub = iota((8, LANES), 0)
    lane_group = lane >> 5
    target = 4 * sub + lane_group
    angle = jnp.zeros((8, LANES), jnp.float32)
    for t in range(LAT_BLOCK):
        angle = jnp.where(target == t, lat_ang[0, 0, 0, t], angle)
    for t in range(LON_BLOCK):
        u, v = (5, t + 1) if t < 3 else (6, t - 3)
        angle = jnp.where(target == 4 * u + v, lon_ang[0, 0, 0, t], angle)
    cos_angle = jnp.cos(angle)
    sin_angle = jnp.sin(angle)

    total_rows = CLAT * n_lat
    inv_lon, inv_sq = [], []
    for h in range(2):
        row = (a * CLAT + 8 * h + sub).astype(jnp.float32)
        cosine = jnp.cos((row + 0.5 - 0.5 * total_rows) * (0.5 * math.pi / total_rows))
        inv_lon.append(1.0 / (60.0 * cosine))
        inv_sq.append(1.0 / (cosine * cosine))

    k_lat = 4 * (iota((32, n_lat), 0) & 7) + (iota((32, n_lat), 0) >> 3) + jnp.where(low_a, 0, n_lat // 2)
    choose_lat = jnp.where(lat_pair[p] == k_lat, 1.0, 0.0)
    choose_lon = jnp.where(lon_pair[p] == iota((CLAT, n_lon), 0), 1.0, 0.0)

    count = 4
    for there, _ in neighbours:
        count = count + jnp.where(there, 1, 0)
    pl.semaphore_wait(barrier, count)

    def halo_copies(s, x):
        inner = pl.ds(1, GROUPS)
        pieces = (
            (x.at[:, inner, pl.ds(TOP, 3), :], x.at[:, inner, pl.ds(TOP + CLAT, 3), :]),
            (x.at[:, inner, pl.ds(TOP + CLAT - 3, 3), :], x.at[:, inner, pl.ds(TOP - 3, 3), :]),
            (x.at[:, 1, pl.ds(TOP, CLAT), :], x.at[:, GROUPS + 1, pl.ds(TOP, CLAT), :]),
            (x.at[:, GROUPS, pl.ds(TOP, CLAT), :], x.at[:, 0, pl.ds(TOP, CLAT), :]),
        )
        copies = []
        for i, ((there, device), (src, dst)) in enumerate(zip(neighbours, pieces)):
            copies.append(
                (
                    there,
                    pltpu.make_async_remote_copy(
                        src_ref=src,
                        dst_ref=dst,
                        send_sem=halo_send.at[s, i],
                        recv_sem=halo_recv.at[s, i],
                        device_id=device,
                        device_id_type=MESH,
                    ),
                )
            )
        return copies

    def rim_copies(s):
        lat_src = zbuf.at[s, :, pl.ds(0, SPAN), :]
        lat_dst = rl.at[s, a]
        ends = (
            (lat_src, lat_dst.at[:, pl.ds(0, SPAN), :], (q, 0, b), 0),
            (lat_src, lat_dst.at[:, pl.ds(0, SPAN), :], (q, n_lat - 1, b), 0),
            (wbuf.at[s, 0], rw.at[s, b], (q, a, 0), 1),
            (wbuf.at[s, 1], rw.at[s, b], (q, a, n_lon - 1), 1),
        )
        return [
            pltpu.make_async_remote_copy(
                src_ref=src,
                dst_ref=dst,
                send_sem=rim_send.at[s, i],
                recv_sem=rim_recv.at[s, kind],
                device_id=device,
                device_id_type=MESH,
            )
            for i, (src, dst, device, kind) in enumerate(ends)
        ]

    def export(s, x):
        columns = []
        for f in range(FIELDS):
            parts = [x[f, g + 1, TOP : TOP + CLAT, :] for g in range(GROUPS)]
            columns.append(jnp.concatenate(parts, axis=0))
        total = dot(mat[...], jnp.concatenate(columns, axis=1))
        blocks = []
        for f in range(FIELDS):
            piece = total[:, f * LANES : (f + 1) * LANES]
            result = None
            for shift in range(4):
                mixed = None
                for kk in range(4):
                    v = (kk + shift) % 4
                    part = piece[kk * 32 + v * 8 : kk * 32 + v * 8 + 8, :]
                    mixed = part if mixed is None else jnp.where(lane_group == kk, part, mixed)
                if shift:
                    mixed = pltpu.roll(mixed, 32 * shift, 1)
                result = mixed if result is None else result + mixed
            blocks.append(result)
        east = cos_angle * blocks[1] + sin_angle * blocks[2]
        north = cos_angle * blocks[2] - sin_angle * blocks[1]
        blocks[1], blocks[2] = east, north
        for f in range(FIELDS):
            zbuf[s, f] = blocks[f]
            wbuf[s, 0, f : f + 1, :] = blocks[f][5:6]
            wbuf[s, 1, f : f + 1, :] = blocks[f][6:7]

    def place_lat(s, x, first_row):
        half = lane < 64
        for f in range(FIELDS):
            got = []
            for u in range(SPAN):
                got.append(jnp.concatenate([rl[s, i, f, u : u + 1, :] for i in range(n_lat)], axis=0))
            placed = dot(choose_lat, jnp.concatenate(got, axis=1))
            for c in range(2):
                plain = [placed[16 * c : 16 * c + 8, u * LANES : (u + 1) * LANES] for u in range(SPAN)]
                moved = [
                    pltpu.roll(placed[16 * c + 8 : 16 * c + 16, u * LANES : (u + 1) * LANES], 64, 1)
                    for u in range(SPAN)
                ]
                tiles = plain[:4] + [jnp.where(half, plain[4], moved[0])]
                tiles += [jnp.where(half, moved[u], moved[u + 1]) for u in range(4)]
                for g, value in enumerate(tiles):
                    x[f, 1 + 9 * c + g, first_row : first_row + 3, :] = value[0:3]

    def place_lon(s, x, group):
        got = []
        for f in range(FIELDS):
            got.append(jnp.concatenate([rw[s, i, f : f + 1, :] for i in range(n_lon)], axis=0))
        placed = dot(choose_lon, jnp.concatenate(got, axis=1))
        for f in range(FIELDS):
            x[f, group, TOP : TOP + CLAT, :] = placed[:, f * LANES : (f + 1) * LANES]

    def receive(s, x):
        lat_got = rl.at[s, :, :, pl.ds(0, SPAN), :]
        lon_got = rw.at[s]

        @pl.when(jnp.logical_or(low_b, high_b))
        def _():
            pltpu.make_async_copy(lon_got, lon_got, rim_recv.at[s, 1]).wait()

        @pl.when(low_b)
        def _():
            place_lon(s, x, 0)

        @pl.when(high_b)
        def _():
            place_lon(s, x, GROUPS + 1)

        @pl.when(jnp.logical_or(low_a, high_a))
        def _():
            pltpu.make_async_copy(lat_got, lat_got, rim_recv.at[s, 0]).wait()

        @pl.when(low_a)
        def _():
            place_lat(s, x, TOP - 3)

        @pl.when(high_a)
        def _():
            place_lat(s, x, TOP + CLAT)

    not_last = (lane & (LEV - 1)) != LEV - 1
    not_first = (lane & (LEV - 1)) != 0

    def derivatives(x, f, g, r, h):
        def row(o):
            return x[f, g, r + o : r + o + 8, :]

        here = row(0)
        west, east = x[f, g - 1, r : r + 8, :], x[f, g + 1, r : r + 8, :]
        up1, down1 = row(1), row(-1)
        lat = (
            0.75 * (up1 - down1) - 0.15 * (row(2) - row(-2)) + (1.0 / 60.0) * (row(3) - row(-3))
        )
        plus1 = pltpu.roll(jnp.where(lane < 32, east, here), 96, 1)
        minus1 = pltpu.roll(jnp.where(lane >= 96, west, here), 32, 1)
        two = pltpu.roll(jnp.where(lane < 64, east - here, here - west), 64, 1)
        plus3 = pltpu.roll(jnp.where(lane < 96, east, here), 32, 1)
        minus3 = pltpu.roll(jnp.where(lane >= 32, west, here), 96, 1)
        lon = (45.0 * (plus1 - minus1) - 9.0 * two + (plus3 - minus3)) * inv_lon[h]
        upper = jnp.where(not_last, pltpu.roll(here, LANES - 1, 1), 0.0)
        lower = jnp.where(not_first, pltpu.roll(here, 1, 1), 0.0)
        lev = 0.5 * (upper - lower)
        lap = up1 + down1 - 2.0 * here + (plus1 + minus1 - 2.0 * here) * inv_sq[h]
        return here, lat, lon, lev, lap

    def section(x, store):
        def step(g, carry):
            begin = pl.multiple_of((g - 1) * LANES, LANES)
            for h in range(2):
                r = TOP + 8 * h
                u = x[1, g, r : r + 8, :]
                v = x[2, g, r : r + 8, :]
                w = x[3, g, r : r + 8, :]
                rho = x[0, g, r : r + 8, :]
                nu = visc[0, 8 * h : 8 * h + 8, pl.ds(begin, LANES)]

                def plain(f):
                    here, lat, lon, lev, lap = derivatives(x, f, g, r, h)
                    return here, lat, lon, lev, nu * lap - (u * lon + v * lat + w * lev)

                e, e_lat, e_lon, e_lev, e_rate = plain(4)
                here, _, lon, _, rate = plain(1)
                div = lon
                store(1, g, h, begin, here, rate - KAPPA_PRESS * e_lon)
                here, lat, _, _, rate = plain(2)
                div = div + lat
                store(2, g, h, begin, here, rate - KAPPA_PRESS * e_lat)
                here, _, _, lev, rate = plain(3)
                div = div + lev
                store(3, g, h, begin, here, rate - KAPPA_PRESS * e_lev - rho)
                here, _, _, _, rate = plain(0)
                store(0, g, h, begin, here, rate - div)
                store(4, g, h, begin, e, e_rate - GAMMA_HEAT * div)
            return carry

        lax.fori_loop(1, GROUPS + 1, step, 0)

    def store_first(f, g, h, begin, here, rate):
        x2[f, g, TOP + 8 * h : TOP + 8 * h + 8, :] = here + TIME_STEP * rate

    def store_second(f, g, h, begin, here, rate):
        before = x1[f, g, TOP + 8 * h : TOP + 8 * h + 8, :]
        out[0, f, 8 * h : 8 * h + 8, pl.ds(begin, LANES)] = 0.5 * (
            before + here + TIME_STEP * rate
        )

    def exchange(s, x):
        halos = halo_copies(s, x)
        for there, copy in halos:

            @pl.when(there)
            def _():
                copy.start()

        export(s, x)
        rims = rim_copies(s)
        for copy in rims:
            copy.start()
        for there, copy in halos:

            @pl.when(there)
            def _():
                copy.wait_send()

        for i in range(4):
            there, _ = neighbours[i]
            copy = halos[i ^ 1][1]

            @pl.when(there)
            def _():
                copy.wait_recv()

        receive(s, x)
        for copy in rims:
            copy.wait_send()

    exchange(0, x1)
    section(x1, store_first)
    exchange(1, x2)
    section(x2, store_second)


def on_device(*operands):
    n_lat = lax.axis_size("lat")
    n_lon = lax.axis_size("lon")
    vmem = pl.BlockSpec(memory_space=pltpu.VMEM)
    smem = pl.BlockSpec(memory_space=pltpu.SMEM)

    def body(*refs):
        kernel(n_lat, n_lon, *refs)

    return pl.pallas_call(
        body,
        out_shape=jax.ShapeDtypeStruct(operands[0].shape, jnp.float32),
        in_specs=[vmem, vmem, vmem, vmem, smem, smem, smem, smem, vmem, vmem],
        out_specs=vmem,
        scratch_shapes=[
            pltpu.VMEM((FIELDS, GROUPS + 2, 32, LANES), jnp.float32),
            pltpu.VMEM((FIELDS, GROUPS + 2, 32, LANES), jnp.float32),
            pltpu.VMEM((2, 32, LANES), jnp.float32),
            pltpu.VMEM((LANES, GROUPS * CLAT), jnp.float32),
            pltpu.VMEM((2, FIELDS, 8, LANES), jnp.float32),
            pltpu.VMEM((2, 2, 8, LANES), jnp.float32),
            pltpu.VMEM((2, n_lat, FIELDS, 8, LANES), jnp.float32),
            pltpu.VMEM((2, n_lon, 8, LANES), jnp.float32),
            pltpu.SemaphoreType.DMA((2, 4)),
            pltpu.SemaphoreType.DMA((2, 4)),
            pltpu.SemaphoreType.DMA((2, 4)),
            pltpu.SemaphoreType.DMA((2, 2)),
        ],
        compiler_params=pltpu.CompilerParams(
            collective_id=0, has_side_effects=True, vmem_limit_bytes=40 * 1024 * 1024
        ),
    )(*operands)


def solution(mesh):
    in_specs = (
        P("yy", None, "lat", "lon"),
        P("yy", "lat", "lon"),
        P("yy", "lat", "lon", None, None),
        P("yy", "lat", "lon", None, None),
        P("yy", "lat", "lon", None),
        P("yy", "lat", "lon", None),
        P("yy", "lat", "lon", None),
        P("yy", "lat", "lon", None),
        P(None, "lon", None),
        P(None, "lat", None),
    )
    out_specs = P("yy", None, "lat", "lon")
    return jax.shard_map(
        on_device, mesh=mesh, in_specs=in_specs, out_specs=out_specs, check_vma=False
    )
```

```python
import math

import jax
import jax.numpy as jnp
from jax import lax
from jax.experimental import pallas as pl
from jax.experimental.pallas import tpu as pltpu
from jax.sharding import PartitionSpec as P

FIELDS = 5
LEV = 32
CLAT = 16
GROUPS = 18
LANES = 128
PATCH_H = 8
PATCH_W = 16
LAT_BLOCK = 18
LON_BLOCK = 6
SPAN = 5
BLOCK_ROWS = 32
TOP = 8

TIME_STEP = 0.2
KAPPA_PRESS = 0.4
GAMMA_HEAT = 1.4

MESH = pl.DeviceIdType.MESH


def dot(left, right):
    return jnp.dot(left, right, preferred_element_type=jnp.float32)


def iota(shape, axis):
    return lax.broadcasted_iota(jnp.int32, shape, axis)


def split(value, parts):
    pieces = []
    for _ in range(parts):
        piece = value.astype(jnp.bfloat16)
        pieces.append(piece)
        value = value - piece.astype(jnp.float32)
    return pieces


def kernel(
    n_lat,
    n_lon,
    fields_hbm,
    visc_hbm,
    lat_w_hbm,
    lon_w_hbm,
    lat_ang_hbm,
    lon_ang_hbm,
    rows_hbm,
    cols_hbm,
    lat_pair_hbm,
    lon_pair_hbm,
    out,
    x1,
    x2,
    visc,
    lat_w,
    lon_w,
    lat_ang,
    lon_ang,
    rows,
    cols,
    lat_pair,
    lon_pair,
    wp,
    mat,
    metric,
    zbuf,
    wbuf,
    rl,
    rw,
    local,
    halo_send,
    halo_recv,
    rim_send,
    rim_recv,
):
    p = lax.axis_index("yy")
    a = lax.axis_index("lat")
    b = lax.axis_index("lon")
    q = 1 - p
    low_a, high_a = a == 0, a == n_lat - 1
    low_b, high_b = b == 0, b == n_lon - 1
    lat_edge = jnp.logical_or(low_a, high_a)
    lon_edge = jnp.logical_or(low_b, high_b)
    neighbours = (
        (jnp.logical_not(low_a), (p, a - 1, b)),
        (jnp.logical_not(high_a), (p, a + 1, b)),
        (jnp.logical_not(low_b), (p, a, b - 1)),
        (jnp.logical_not(high_b), (p, a, b + 1)),
    )

    small = [
        pltpu.make_async_copy(src, dst, local.at[i])
        for i, (src, dst) in enumerate(
            (
                (lat_w_hbm, lat_w),
                (lon_w_hbm, lon_w),
                (lat_ang_hbm, lat_ang),
                (lon_ang_hbm, lon_ang),
                (rows_hbm, rows),
                (cols_hbm, cols),
                (lat_pair_hbm, lat_pair),
                (lon_pair_hbm, lon_pair),
                (visc_hbm, visc),
            )
        )
    ]
    for copy in small[:6]:
        copy.start()
    inner = pl.ds(1, GROUPS)
    for g in range(GROUPS):
        pltpu.make_async_copy(
            fields_hbm.at[0, :, :, pl.ds(g * LANES, LANES)],
            x1.at[:, g + 1, pl.ds(TOP, CLAT), :],
            local.at[9],
        ).start()
    for copy in small[6:]:
        copy.start()

    barrier = pltpu.get_barrier_semaphore()
    for there, device in neighbours:

        @pl.when(there)
        def _():
            pl.semaphore_signal(barrier, inc=1, device_id=device, device_id_type=MESH)

    @pl.when(lat_edge)
    def _():
        def one(i, carry):
            pl.semaphore_signal(barrier, inc=1, device_id=(q, i, b), device_id_type=MESH)
            return carry

        lax.fori_loop(0, n_lat, one, 0)

    @pl.when(lon_edge)
    def _():
        def one(i, carry):
            pl.semaphore_signal(barrier, inc=1, device_id=(q, a, i), device_id_type=MESH)
            return carry

        lax.fori_loop(0, n_lon, one, 0)

    wp[...] = jnp.zeros_like(wp)
    for copy in small[:6]:
        copy.wait()
    for t in range(LAT_BLOCK):
        u, v = t // 4, t % 4
        wp[v * 8 + u : v * 8 + u + 1, 0:LANES] = lat_w[t]
    for t in range(LON_BLOCK):
        u, v = (5, t + 1) if t < 3 else (6, t - 3)
        wp[v * 8 + u : v * 8 + u + 1, LANES : 2 * LANES] = lon_w[t]
    weights = jnp.concatenate(split(wp[...], 3), axis=0)
    entry = iota((2 * LANES, GROUPS * CLAT), 0)
    place = iota((2 * LANES, GROUPS * CLAT), 1)
    is_lon = entry >= LANES
    entry = entry & (LANES - 1)
    row0 = jnp.where(is_lon, rows[0, 0, 0, 1], rows[0, 0, 0, 0])
    col0 = jnp.where(is_lon, cols[0, 0, 0, 1], cols[0, 0, 0, 0])
    from_col = (entry & (PATCH_W - 1)) - 4 * (place >> 4) + col0
    same_row = (place & (CLAT - 1)) - (entry >> 4) == row0
    from_col = jnp.where(same_row, from_col, -1)
    for kk in range(4):
        chosen = jnp.where(from_col == kk, 1.0, 0.0).astype(jnp.bfloat16)
        parts = dot(weights, chosen)
        part = parts[0:32] + parts[32:64] + parts[64:96]
        high, low = split(part, 2)
        mat[0, kk * 32 : (kk + 1) * 32, :] = high
        mat[1, kk * 32 : (kk + 1) * 32, :] = low

    lane = iota((8, LANES), 1)
    sub = iota((8, LANES), 0)
    lane_group = lane >> 5
    target = 4 * sub + lane_group
    angle = jnp.zeros((8, LANES), jnp.float32)
    for t in range(LAT_BLOCK):
        angle = jnp.where(target == t, lat_ang[0, 0, 0, t], angle)
    for t in range(LON_BLOCK):
        u, v = (5, t + 1) if t < 3 else (6, t - 3)
        angle = jnp.where(target == 4 * u + v, lon_ang[0, 0, 0, t], angle)
    cos_angle = jnp.cos(angle)
    sin_angle = jnp.sin(angle)

    def export(s, x):
        columns = []
        for f in range(FIELDS):
            columns.append(x[f, 1 : GROUPS + 1, TOP : TOP + CLAT, :].reshape(GROUPS * CLAT, LANES))
        high, low = split(jnp.concatenate(columns, axis=1), 2)
        total = dot(mat[0], high) + dot(mat[0], low) + dot(mat[1], high)
        blocks = []
        for f in range(FIELDS):
            piece = total[:, f * LANES : (f + 1) * LANES]
            result = None
            for shift in range(4):
                mixed = None
                for kk in range(4):
                    v = (kk + shift) % 4
                    part = piece[kk * 32 + v * 8 : kk * 32 + v * 8 + 8, :]
                    mixed = part if mixed is None else jnp.where(lane_group == kk, part, mixed)
                if shift:
                    mixed = pltpu.roll(mixed, 32 * shift, 1)
                result = mixed if result is None else result + mixed
            blocks.append(result)
        east = cos_angle * blocks[1] + sin_angle * blocks[2]
        north = cos_angle * blocks[2] - sin_angle * blocks[1]
        blocks[1], blocks[2] = east, north
        for f in range(FIELDS):
            zbuf[s, SPAN * f : SPAN * f + SPAN, :] = blocks[f][0:SPAN]
            wbuf[s, 0, f : f + 1, :] = blocks[f][5:6]
            wbuf[s, 1, f : f + 1, :] = blocks[f][6:7]

    def rim_copies(s):
        lat_dst = rl.at[pl.ds((s * n_lat + a) * BLOCK_ROWS, BLOCK_ROWS), :]
        lon_dst = rw.at[pl.ds((s * n_lon + b) * 8, 8), :]
        ends = (
            (zbuf.at[s], lat_dst, (q, 0, b), 0),
            (zbuf.at[s], lat_dst, (q, n_lat - 1, b), 0),
            (wbuf.at[s, 0], lon_dst, (q, a, 0), 1),
            (wbuf.at[s, 1], lon_dst, (q, a, n_lon - 1), 1),
        )
        return [
            pltpu.make_async_remote_copy(
                src_ref=src,
                dst_ref=dst,
                send_sem=rim_send.at[s, i],
                recv_sem=rim_recv.at[s, kind],
                device_id=device,
                device_id_type=MESH,
            )
            for i, (src, dst, device, kind) in enumerate(ends)
        ]

    def row_copy(s, x, h):
        there = jnp.where(h == 0, jnp.logical_not(low_a), jnp.logical_not(high_a))
        return there, pltpu.make_async_remote_copy(
            src_ref=x.at[:, inner, pl.ds(TOP + (CLAT - 3) * h, 3), :],
            dst_ref=x.at[:, inner, pl.ds(TOP + CLAT - (CLAT + 3) * h, 3), :],
            send_sem=halo_send.at[s, 0, h],
            recv_sem=halo_recv.at[s, 0, h],
            device_id=(p, a + 2 * h - 1, b),
            device_id_type=MESH,
        )

    def col_copies(s, x, h):
        band = pl.ds(pl.multiple_of(TOP + 8 * h, 8), 8)
        ends = ((1, GROUPS + 1), (GROUPS, 0))
        return [
            (
                neighbours[2 + i][0],
                pltpu.make_async_remote_copy(
                    src_ref=x.at[:, src, band, :],
                    dst_ref=x.at[:, dst, band, :],
                    send_sem=halo_send.at[s, 1 + i, h],
                    recv_sem=halo_recv.at[s, 1 + i, h],
                    device_id=neighbours[2 + i][1],
                    device_id_type=MESH,
                ),
            )
            for i, (src, dst) in enumerate(ends)
        ]

    def send_half(s, x, h):
        for there, copy in [row_copy(s, x, h)] + col_copies(s, x, h):

            @pl.when(there)
            def _():
                copy.start()

    pltpu.make_async_copy(
        x1.at[:, inner, pl.ds(TOP, CLAT), :], x1.at[:, inner, pl.ds(TOP, CLAT), :], local.at[9]
    ).wait()
    export(0, x1)

    count = 4
    for there, _ in neighbours:
        count = count + jnp.where(there, 1, 0)
    pl.semaphore_wait(barrier, count)

    for copy in rim_copies(0):
        copy.start()
    for h in range(2):
        send_half(0, x1, h)

    for copy in small[6:]:
        copy.wait()
    total_rows = CLAT * n_lat
    for h in range(2):
        row = (a * CLAT + 8 * h + sub).astype(jnp.float32)
        cosine = jnp.cos((row + 0.5 - 0.5 * total_rows) * (0.5 * math.pi / total_rows))
        metric[h, 0] = 1.0 / (60.0 * cosine)
        metric[h, 1] = 1.0 / (cosine * cosine)

    k_lat = (
        4 * (iota((32, n_lat), 0) & 7)
        + (iota((32, n_lat), 0) >> 3)
        + jnp.where(low_a, 0, n_lat // 2)
    )
    choose_lat = jnp.where(lat_pair[p] == k_lat, 1.0, 0.0).astype(jnp.bfloat16)
    choose_lon = jnp.where(lon_pair[p] == iota((CLAT, n_lon), 0), 1.0, 0.0).astype(jnp.bfloat16)

    def place_lat(s, x, first_row):
        half = lane < 64
        for f in range(FIELDS):
            got = jnp.concatenate(
                [
                    rl[pl.ds(s * n_lat * BLOCK_ROWS + SPAN * f + u, n_lat, stride=BLOCK_ROWS), :]
                    for u in range(SPAN)
                ],
                axis=1,
            )
            placed = None
            for piece in split(got, 3):
                term = dot(choose_lat, piece)
                placed = term if placed is None else placed + term
            for c in range(2):
                plain = [placed[16 * c : 16 * c + 8, u * LANES : (u + 1) * LANES] for u in range(SPAN)]
                moved = [
                    pltpu.roll(placed[16 * c + 8 : 16 * c + 16, u * LANES : (u + 1) * LANES], 64, 1)
                    for u in range(SPAN)
                ]
                tiles = plain[:4] + [jnp.where(half, plain[4], moved[0])]
                tiles += [jnp.where(half, moved[u], moved[u + 1]) for u in range(4)]
                for g, value in enumerate(tiles):
                    x[f, 1 + 9 * c + g, first_row : first_row + 3, :] = value[0:3]

    def place_lon(s, x, group):
        got = jnp.concatenate(
            [rw[pl.ds(s * n_lon * 8 + f, n_lon, stride=8), :] for f in range(FIELDS)], axis=1
        )
        placed = None
        for piece in split(got, 3):
            term = dot(choose_lon, piece)
            placed = term if placed is None else placed + term
        for f in range(FIELDS):
            x[f, group, TOP : TOP + CLAT, :] = placed[:, f * LANES : (f + 1) * LANES]

    def wait_rows(s, x, h):
        there = jnp.where(h == 0, jnp.logical_not(low_a), jnp.logical_not(high_a))

        @pl.when(there)
        def _():
            row_copy(s, x, 1 - h)[1].wait_recv()

        @pl.when(jnp.logical_not(there))
        def _():
            got = rl.at[pl.ds(s * n_lat * BLOCK_ROWS, n_lat * BLOCK_ROWS), :]
            pltpu.make_async_copy(got, got, rim_recv.at[s, 0]).wait()

        @pl.when(jnp.logical_and(h == 0, low_a))
        def _():
            place_lat(s, x, TOP - 3)

        @pl.when(jnp.logical_and(h == 1, high_a))
        def _():
            place_lat(s, x, TOP + CLAT)

    def wait_cols(s, x):
        for h in range(2):
            (west, to_west), (east, to_east) = col_copies(s, x, h)

            @pl.when(west)
            def _():
                to_east.wait_recv()

            @pl.when(east)
            def _():
                to_west.wait_recv()

        @pl.when(lon_edge)
        def _():
            got = rw.at[pl.ds(s * n_lon * 8, n_lon * 8), :]
            pltpu.make_async_copy(got, got, rim_recv.at[s, 1]).wait()

        @pl.when(low_b)
        def _():
            place_lon(s, x, 0)

        @pl.when(high_b)
        def _():
            place_lon(s, x, GROUPS + 1)

    not_last = (lane & (LEV - 1)) != LEV - 1
    not_first = (lane & (LEV - 1)) != 0

    def derivatives(x, f, g, r):
        def row(o):
            return x[f, g, pl.ds(r + o, 8), :]

        here = row(0)
        west, east = x[f, g - 1, pl.ds(r, 8), :], x[f, g + 1, pl.ds(r, 8), :]
        up1, down1 = row(1), row(-1)
        lat = (
            0.75 * (up1 - down1) - 0.15 * (row(2) - row(-2)) + (1.0 / 60.0) * (row(3) - row(-3))
        )
        plus1 = pltpu.roll(jnp.where(lane < 32, east, here), 96, 1)
        minus1 = pltpu.roll(jnp.where(lane >= 96, west, here), 32, 1)
        two = pltpu.roll(jnp.where(lane < 64, east - here, here - west), 64, 1)
        plus3 = pltpu.roll(jnp.where(lane < 96, east, here), 32, 1)
        minus3 = pltpu.roll(jnp.where(lane >= 32, west, here), 96, 1)
        lon = 45.0 * (plus1 - minus1) - 9.0 * two + (plus3 - minus3)
        upper = jnp.where(not_last, pltpu.roll(here, LANES - 1, 1), 0.0)
        lower = jnp.where(not_first, pltpu.roll(here, 1, 1), 0.0)
        return here, lat, lon, upper - lower, up1 + down1, plus1 + minus1

    def group_rates(x, g, h, store):
        r = pl.multiple_of(TOP + 8 * h, 8)
        begin = pl.multiple_of((g - 1) * LANES, LANES)
        inv_lon, inv_sq = metric[h, 0], metric[h, 1]
        centre = 2.0 + 2.0 * inv_sq
        u = x[1, g, pl.ds(r, 8), :] * inv_lon
        v = x[2, g, pl.ds(r, 8), :]
        w = x[3, g, pl.ds(r, 8), :] * 0.5
        rho = x[0, g, pl.ds(r, 8), :]
        nu = visc[0, pl.ds(pl.multiple_of(8 * h, 8), 8), pl.ds(begin, LANES)]

        def plain(f):
            here, lat, lon, lev, rows_sum, cols_sum = derivatives(x, f, g, r)
            lap = rows_sum + cols_sum * inv_sq - centre * here
            return here, lat, lon, lev, nu * lap - (u * lon + v * lat + w * lev)

        e, e_lat, e_lon, e_lev, e_rate = plain(4)
        here, _, lon, _, rate = plain(1)
        div = lon * inv_lon
        store(1, g, h, begin, here, rate - KAPPA_PRESS * (e_lon * inv_lon))
        here, lat, _, _, rate = plain(2)
        div = div + lat
        store(2, g, h, begin, here, rate - KAPPA_PRESS * e_lat)
        here, _, _, lev, rate = plain(3)
        div = div + 0.5 * lev
        store(3, g, h, begin, here, rate - (0.5 * KAPPA_PRESS) * e_lev - rho)
        here, _, _, _, rate = plain(0)
        store(0, g, h, begin, here, rate - div)
        store(4, g, h, begin, e, e_rate - GAMMA_HEAT * div)

    def section(s, x, store):
        first_half = jnp.where(low_a, 1, 0)

        def block(i, carry):
            second = jnp.where(lat_edge, i // 2, i % 2)
            cols_part = jnp.where(lat_edge, i % 2, i // 2)
            h = jnp.where(second == 0, first_half, 1 - first_half)

            @pl.when(cols_part == 0)
            def _():
                wait_rows(s, x, h)

            @pl.when(jnp.logical_and(cols_part == 1, second == 0))
            def _():
                wait_cols(s, x)

            def step(k, inside):
                for one in range(2):
                    g = jnp.where(cols_part == 0, 2 + 2 * k + one, 1 + (GROUPS - 1) * one)
                    group_rates(x, g, h, store)
                return inside

            lax.fori_loop(0, jnp.where(cols_part == 0, (GROUPS - 2) // 2, 1), step, 0)
            if s == 0:

                @pl.when(cols_part == 1)
                def _():
                    send_half(1, x2, h)

            return carry

        lax.fori_loop(0, 4, block, 0)

    def store_first(f, g, h, begin, here, rate):
        x2[f, g, pl.ds(pl.multiple_of(TOP + 8 * h, 8), 8), :] = here + TIME_STEP * rate

    def store_second(f, g, h, begin, here, rate):
        before = x1[f, g, pl.ds(pl.multiple_of(TOP + 8 * h, 8), 8), :]
        out[0, f, pl.ds(pl.multiple_of(8 * h, 8), 8), pl.ds(begin, LANES)] = 0.5 * (
            before + here + TIME_STEP * rate
        )

    section(0, x1, store_first)
    export(1, x2)
    for copy in rim_copies(1):
        copy.start()
    section(1, x2, store_second)

    for s, x in enumerate((x1, x2)):
        for copy in rim_copies(s):
            copy.wait_send()
        for h in range(2):
            for there, copy in [row_copy(s, x, h)] + col_copies(s, x, h):

                @pl.when(there)
                def _():
                    copy.wait_send()


def on_device(*operands):
    n_lat = lax.axis_size("lat")
    n_lon = lax.axis_size("lon")
    operands = list(operands)
    operands[2] = operands[2].reshape(LAT_BLOCK, 1, LANES)
    operands[3] = operands[3].reshape(LON_BLOCK, 1, LANES)

    def body(*refs):
        kernel(n_lat, n_lon, *refs)

    def vmem(*shape):
        return pltpu.VMEM(shape, jnp.float32)

    return pl.pallas_call(
        body,
        out_shape=jax.ShapeDtypeStruct(operands[0].shape, jnp.float32),
        in_specs=[pl.BlockSpec(memory_space=pltpu.HBM)] * 10,
        out_specs=pl.BlockSpec(memory_space=pltpu.VMEM),
        scratch_shapes=[
            vmem(FIELDS, GROUPS + 2, 32, LANES),
            vmem(FIELDS, GROUPS + 2, 32, LANES),
            vmem(1, CLAT, GROUPS * LANES),
            vmem(LAT_BLOCK, 1, LANES),
            vmem(LON_BLOCK, 1, LANES),
            pltpu.SMEM((1, 1, 1, LAT_BLOCK), jnp.float32),
            pltpu.SMEM((1, 1, 1, LON_BLOCK), jnp.float32),
            pltpu.SMEM((1, 1, 1, 2), jnp.int32),
            pltpu.SMEM((1, 1, 1, 2), jnp.int32),
            pltpu.VMEM((2, 1, n_lat), jnp.int32),
            pltpu.VMEM((2, 1, n_lon), jnp.int32),
            vmem(32, 2 * LANES),
            pltpu.VMEM((2, LANES, GROUPS * CLAT), jnp.bfloat16),
            vmem(2, 2, 8, LANES),
            vmem(2, BLOCK_ROWS, LANES),
            vmem(2, 2, 8, LANES),
            vmem(2 * n_lat * BLOCK_ROWS, LANES),
            vmem(2 * n_lon * 8, LANES),
            pltpu.SemaphoreType.DMA((10,)),
            pltpu.SemaphoreType.DMA((2, 3, 2)),
            pltpu.SemaphoreType.DMA((2, 3, 2)),
            pltpu.SemaphoreType.DMA((2, 4)),
            pltpu.SemaphoreType.DMA((2, 2)),
        ],
        compiler_params=pltpu.CompilerParams(
            collective_id=0, has_side_effects=True, vmem_limit_bytes=56 * 1024 * 1024
        ),
    )(*operands)


def solution(mesh):
    in_specs = (
        P("yy", None, "lat", "lon"),
        P("yy", "lat", "lon"),
        P("yy", "lat", "lon", None, None),
        P("yy", "lat", "lon", None, None),
        P("yy", "lat", "lon", None),
        P("yy", "lat", "lon", None),
        P("yy", "lat", "lon", None),
        P("yy", "lat", "lon", None),
        P(None, "lon", None),
        P(None, "lat", None),
    )
    out_specs = P("yy", None, "lat", "lon")
    return jax.shard_map(
        on_device, mesh=mesh, in_specs=in_specs, out_specs=out_specs, check_vma=False
    )
```

```python
import math

import jax
import jax.numpy as jnp
from jax import lax
from jax.experimental import pallas as pl
from jax.experimental.pallas import tpu as pltpu
from jax.sharding import PartitionSpec as P

FIELDS = 5
LEV = 32
CLAT = 16
GROUPS = 18
LANES = 128
PATCH_H = 8
PATCH_W = 16
LAT_BLOCK = 18
LON_BLOCK = 6
SPAN = 5
BLOCK_ROWS = 32
TOP = 8

TIME_STEP = 0.2
KAPPA_PRESS = 0.4
GAMMA_HEAT = 1.4

MESH = pl.DeviceIdType.MESH


def dot(left, right):
    return jnp.dot(left, right, preferred_element_type=jnp.float32)


def iota(shape, axis):
    return lax.broadcasted_iota(jnp.int32, shape, axis)


def split(value, parts):
    pieces = []
    for _ in range(parts):
        piece = value.astype(jnp.bfloat16)
        pieces.append(piece)
        value = value - piece.astype(jnp.float32)
    return pieces


def kernel(
    n_lat,
    n_lon,
    fields_hbm,
    visc_hbm,
    lat_w_hbm,
    lon_w_hbm,
    lat_ang_hbm,
    lon_ang_hbm,
    rows_hbm,
    cols_hbm,
    lat_pair_hbm,
    lon_pair_hbm,
    out,
    x1,
    x2,
    visc,
    lat_w,
    lon_w,
    lat_ang,
    lon_ang,
    rows,
    cols,
    lat_pair,
    lon_pair,
    wp,
    mat,
    metric,
    zbuf,
    wbuf,
    rl,
    rw,
    local,
    halo_send,
    halo_recv,
    rim_send,
    rim_recv,
):
    p = lax.axis_index("yy")
    a = lax.axis_index("lat")
    b = lax.axis_index("lon")
    q = 1 - p
    low_a, high_a = a == 0, a == n_lat - 1
    low_b, high_b = b == 0, b == n_lon - 1
    lat_edge = jnp.logical_or(low_a, high_a)
    lon_edge = jnp.logical_or(low_b, high_b)
    neighbours = (
        (jnp.logical_not(low_a), (p, a - 1, b)),
        (jnp.logical_not(high_a), (p, a + 1, b)),
        (jnp.logical_not(low_b), (p, a, b - 1)),
        (jnp.logical_not(high_b), (p, a, b + 1)),
    )

    barrier = pltpu.get_barrier_semaphore()
    for there, device in neighbours:

        @pl.when(there)
        def _():
            pl.semaphore_signal(barrier, inc=1, device_id=device, device_id_type=MESH)

    @pl.when(lat_edge)
    def _():
        def one(i, carry):
            pl.semaphore_signal(barrier, inc=1, device_id=(q, i, b), device_id_type=MESH)
            return carry

        lax.fori_loop(0, n_lat, one, 0)

    @pl.when(lon_edge)
    def _():
        def one(i, carry):
            pl.semaphore_signal(barrier, inc=1, device_id=(q, a, i), device_id_type=MESH)
            return carry

        lax.fori_loop(0, n_lon, one, 0)

    small = [
        pltpu.make_async_copy(src, dst, local.at[i])
        for i, (src, dst) in enumerate(
            (
                (lat_w_hbm, lat_w),
                (lon_w_hbm, lon_w),
                (lat_ang_hbm, lat_ang),
                (lon_ang_hbm, lon_ang),
                (rows_hbm, rows),
                (cols_hbm, cols),
                (lat_pair_hbm, lat_pair),
                (lon_pair_hbm, lon_pair),
                (visc_hbm, visc),
            )
        )
    ]
    for copy in small[:6]:
        copy.start()
    inner = pl.ds(1, GROUPS)
    for g in range(GROUPS):
        pltpu.make_async_copy(
            fields_hbm.at[0, :, :, pl.ds(g * LANES, LANES)],
            x1.at[:, g + 1, pl.ds(TOP, CLAT), :],
            local.at[9],
        ).start()
    for copy in small[6:]:
        copy.start()

    wp[...] = jnp.zeros_like(wp)
    for copy in small[:6]:
        copy.wait()
    for t in range(LAT_BLOCK):
        u, v = t // 4, t % 4
        wp[v * 8 + u : v * 8 + u + 1, 0:LANES] = lat_w[t]
    for t in range(LON_BLOCK):
        u, v = (5, t + 1) if t < 3 else (6, t - 3)
        wp[v * 8 + u : v * 8 + u + 1, LANES : 2 * LANES] = lon_w[t]
    weights = jnp.concatenate(split(wp[...], 3), axis=0)
    entry = iota((2 * LANES, GROUPS * CLAT), 0)
    place = iota((2 * LANES, GROUPS * CLAT), 1)
    is_lon = entry >= LANES
    entry = entry & (LANES - 1)
    row0 = jnp.where(is_lon, rows[0, 0, 0, 1], rows[0, 0, 0, 0])
    col0 = jnp.where(is_lon, cols[0, 0, 0, 1], cols[0, 0, 0, 0])
    from_col = (entry & (PATCH_W - 1)) - 4 * (place >> 4) + col0
    same_row = (place & (CLAT - 1)) - (entry >> 4) == row0
    from_col = jnp.where(same_row, from_col, -1)
    for kk in range(4):
        chosen = jnp.where(from_col == kk, 1.0, 0.0).astype(jnp.bfloat16)
        parts = dot(weights, chosen)
        part = parts[0:32] + parts[32:64] + parts[64:96]
        high, low = split(part, 2)
        mat[0, kk * 32 : (kk + 1) * 32, :] = high
        mat[1, kk * 32 : (kk + 1) * 32, :] = low

    lane = iota((8, LANES), 1)
    sub = iota((8, LANES), 0)
    lane_group = lane >> 5
    target = 4 * sub + lane_group
    angle = jnp.zeros((8, LANES), jnp.float32)
    for t in range(LAT_BLOCK):
        angle = jnp.where(target == t, lat_ang[0, 0, 0, t], angle)
    for t in range(LON_BLOCK):
        u, v = (5, t + 1) if t < 3 else (6, t - 3)
        angle = jnp.where(target == 4 * u + v, lon_ang[0, 0, 0, t], angle)
    cos_angle = jnp.cos(angle)
    sin_angle = jnp.sin(angle)

    def export(s, x):
        columns = []
        for f in range(FIELDS):
            columns.append(x[f, 1 : GROUPS + 1, TOP : TOP + CLAT, :].reshape(GROUPS * CLAT, LANES))
        high, low = split(jnp.concatenate(columns, axis=1), 2)
        total = dot(mat[0], high) + dot(mat[0], low) + dot(mat[1], high)
        blocks = []
        for f in range(FIELDS):
            piece = total[:, f * LANES : (f + 1) * LANES]
            result = None
            for shift in range(4):
                mixed = None
                for kk in range(4):
                    v = (kk + shift) % 4
                    part = piece[kk * 32 + v * 8 : kk * 32 + v * 8 + 8, :]
                    mixed = part if mixed is None else jnp.where(lane_group == kk, part, mixed)
                if shift:
                    mixed = pltpu.roll(mixed, 32 * shift, 1)
                result = mixed if result is None else result + mixed
            blocks.append(result)
        east = cos_angle * blocks[1] + sin_angle * blocks[2]
        north = cos_angle * blocks[2] - sin_angle * blocks[1]
        blocks[1], blocks[2] = east, north
        for f in range(FIELDS):
            zbuf[s, SPAN * f : SPAN * f + SPAN, :] = blocks[f][0:SPAN]
            wbuf[s, 0, f : f + 1, :] = blocks[f][5:6]
            wbuf[s, 1, f : f + 1, :] = blocks[f][6:7]

    def rim_copies(s):
        lat_dst = rl.at[pl.ds((s * n_lat + a) * BLOCK_ROWS, BLOCK_ROWS), :]
        lon_dst = rw.at[pl.ds((s * n_lon + b) * 8, 8), :]
        ends = (
            (zbuf.at[s], lat_dst, (q, 0, b), 0),
            (zbuf.at[s], lat_dst, (q, n_lat - 1, b), 0),
            (wbuf.at[s, 0], lon_dst, (q, a, 0), 1),
            (wbuf.at[s, 1], lon_dst, (q, a, n_lon - 1), 1),
        )
        return [
            pltpu.make_async_remote_copy(
                src_ref=src,
                dst_ref=dst,
                send_sem=rim_send.at[s, i],
                recv_sem=rim_recv.at[s, kind],
                device_id=device,
                device_id_type=MESH,
            )
            for i, (src, dst, device, kind) in enumerate(ends)
        ]

    def row_copy(s, x, h):
        there = jnp.where(h == 0, jnp.logical_not(low_a), jnp.logical_not(high_a))
        return there, pltpu.make_async_remote_copy(
            src_ref=x.at[:, inner, pl.ds(TOP + (CLAT - 3) * h, 3), :],
            dst_ref=x.at[:, inner, pl.ds(TOP + CLAT - (CLAT + 3) * h, 3), :],
            send_sem=halo_send.at[s, 0, h],
            recv_sem=halo_recv.at[s, 0, h],
            device_id=(p, a + 2 * h - 1, b),
            device_id_type=MESH,
        )

    def col_copies(s, x, h):
        band = pl.ds(pl.multiple_of(TOP + 8 * h, 8), 8)
        ends = ((1, GROUPS + 1), (GROUPS, 0))
        return [
            (
                neighbours[2 + i][0],
                pltpu.make_async_remote_copy(
                    src_ref=x.at[:, src, band, :],
                    dst_ref=x.at[:, dst, band, :],
                    send_sem=halo_send.at[s, 1 + i, h],
                    recv_sem=halo_recv.at[s, 1 + i, h],
                    device_id=neighbours[2 + i][1],
                    device_id_type=MESH,
                ),
            )
            for i, (src, dst) in enumerate(ends)
        ]

    def send_half(s, x, h):
        for there, copy in [row_copy(s, x, h)] + col_copies(s, x, h):

            @pl.when(there)
            def _():
                copy.start()

    pltpu.make_async_copy(
        x1.at[:, inner, pl.ds(TOP, CLAT), :], x1.at[:, inner, pl.ds(TOP, CLAT), :], local.at[9]
    ).wait()
    export(0, x1)

    count = 4
    for there, _ in neighbours:
        count = count + jnp.where(there, 1, 0)
    pl.semaphore_wait(barrier, count)

    for copy in rim_copies(0):
        copy.start()
    for h in range(2):
        send_half(0, x1, h)

    for copy in small[6:]:
        copy.wait()
    total_rows = CLAT * n_lat
    for h in range(2):
        row = (a * CLAT + 8 * h + sub).astype(jnp.float32)
        cosine = jnp.cos((row + 0.5 - 0.5 * total_rows) * (0.5 * math.pi / total_rows))
        metric[h, 0] = 1.0 / (60.0 * cosine)
        metric[h, 1] = 1.0 / (cosine * cosine)

    k_lat = (
        4 * (iota((32, n_lat), 0) & 7)
        + (iota((32, n_lat), 0) >> 3)
        + jnp.where(low_a, 0, n_lat // 2)
    )
    choose_lat = jnp.where(lat_pair[p] == k_lat, 1.0, 0.0).astype(jnp.bfloat16)
    choose_lon = jnp.where(lon_pair[p] == iota((CLAT, n_lon), 0), 1.0, 0.0).astype(jnp.bfloat16)

    def place_lat(s, x, first_row):
        half = lane < 64
        for f in range(FIELDS):
            got = jnp.concatenate(
                [
                    rl[pl.ds(s * n_lat * BLOCK_ROWS + SPAN * f + u, n_lat, stride=BLOCK_ROWS), :]
                    for u in range(SPAN)
                ],
                axis=1,
            )
            placed = None
            for piece in split(got, 3):
                term = dot(choose_lat, piece)
                placed = term if placed is None else placed + term
            for c in range(2):
                plain = [placed[16 * c : 16 * c + 8, u * LANES : (u + 1) * LANES] for u in range(SPAN)]
                moved = [
                    pltpu.roll(placed[16 * c + 8 : 16 * c + 16, u * LANES : (u + 1) * LANES], 64, 1)
                    for u in range(SPAN)
                ]
                tiles = plain[:4] + [jnp.where(half, plain[4], moved[0])]
                tiles += [jnp.where(half, moved[u], moved[u + 1]) for u in range(4)]
                for g, value in enumerate(tiles):
                    x[f, 1 + 9 * c + g, first_row : first_row + 3, :] = value[0:3]

    def place_lon(s, x, group):
        got = jnp.concatenate(
            [rw[pl.ds(s * n_lon * 8 + f, n_lon, stride=8), :] for f in range(FIELDS)], axis=1
        )
        placed = None
        for piece in split(got, 3):
            term = dot(choose_lon, piece)
            placed = term if placed is None else placed + term
        for f in range(FIELDS):
            x[f, group, TOP : TOP + CLAT, :] = placed[:, f * LANES : (f + 1) * LANES]

    def wait_rows(s, x, h):
        there = jnp.where(h == 0, jnp.logical_not(low_a), jnp.logical_not(high_a))

        @pl.when(there)
        def _():
            row_copy(s, x, 1 - h)[1].wait_recv()

        @pl.when(jnp.logical_not(there))
        def _():
            got = rl.at[pl.ds(s * n_lat * BLOCK_ROWS, n_lat * BLOCK_ROWS), :]
            pltpu.make_async_copy(got, got, rim_recv.at[s, 0]).wait()

        @pl.when(jnp.logical_and(h == 0, low_a))
        def _():
            place_lat(s, x, TOP - 3)

        @pl.when(jnp.logical_and(h == 1, high_a))
        def _():
            place_lat(s, x, TOP + CLAT)

    def wait_cols(s, x):
        for h in range(2):
            (west, to_west), (east, to_east) = col_copies(s, x, h)

            @pl.when(west)
            def _():
                to_east.wait_recv()

            @pl.when(east)
            def _():
                to_west.wait_recv()

        @pl.when(lon_edge)
        def _():
            got = rw.at[pl.ds(s * n_lon * 8, n_lon * 8), :]
            pltpu.make_async_copy(got, got, rim_recv.at[s, 1]).wait()

        @pl.when(low_b)
        def _():
            place_lon(s, x, 0)

        @pl.when(high_b)
        def _():
            place_lon(s, x, GROUPS + 1)

    not_last = (lane & (LEV - 1)) != LEV - 1
    not_first = (lane & (LEV - 1)) != 0

    def derivatives(x, f, g, r):
        def row(o):
            return x[f, g, pl.ds(r + o, 8), :]

        here = row(0)
        west, east = x[f, g - 1, pl.ds(r, 8), :], x[f, g + 1, pl.ds(r, 8), :]
        up1, down1 = row(1), row(-1)
        lat = (
            0.75 * (up1 - down1) - 0.15 * (row(2) - row(-2)) + (1.0 / 60.0) * (row(3) - row(-3))
        )
        plus1 = pltpu.roll(jnp.where(lane < 32, east, here), 96, 1)
        minus1 = pltpu.roll(jnp.where(lane >= 96, west, here), 32, 1)
        two = pltpu.roll(jnp.where(lane < 64, east - here, here - west), 64, 1)
        plus3 = pltpu.roll(jnp.where(lane < 96, east, here), 32, 1)
        minus3 = pltpu.roll(jnp.where(lane >= 32, west, here), 96, 1)
        lon = 45.0 * (plus1 - minus1) - 9.0 * two + (plus3 - minus3)
        upper = jnp.where(not_last, pltpu.roll(here, LANES - 1, 1), 0.0)
        lower = jnp.where(not_first, pltpu.roll(here, 1, 1), 0.0)
        return here, lat, lon, upper - lower, up1 + down1, plus1 + minus1

    def group_rates(x, g, h, store):
        r = pl.multiple_of(TOP + 8 * h, 8)
        begin = pl.multiple_of((g - 1) * LANES, LANES)
        inv_lon, inv_sq = metric[h, 0], metric[h, 1]
        centre = 2.0 + 2.0 * inv_sq
        u = x[1, g, pl.ds(r, 8), :] * inv_lon
        v = x[2, g, pl.ds(r, 8), :]
        w = x[3, g, pl.ds(r, 8), :] * 0.5
        rho = x[0, g, pl.ds(r, 8), :]
        nu = visc[0, pl.ds(pl.multiple_of(8 * h, 8), 8), pl.ds(begin, LANES)]

        def plain(f):
            here, lat, lon, lev, rows_sum, cols_sum = derivatives(x, f, g, r)
            lap = rows_sum + cols_sum * inv_sq - centre * here
            return here, lat, lon, lev, nu * lap - (u * lon + v * lat + w * lev)

        e, e_lat, e_lon, e_lev, e_rate = plain(4)
        here, _, lon, _, rate = plain(1)
        div = lon * inv_lon
        store(1, g, h, begin, here, rate - KAPPA_PRESS * (e_lon * inv_lon))
        here, lat, _, _, rate = plain(2)
        div = div + lat
        store(2, g, h, begin, here, rate - KAPPA_PRESS * e_lat)
        here, _, _, lev, rate = plain(3)
        div = div + 0.5 * lev
        store(3, g, h, begin, here, rate - (0.5 * KAPPA_PRESS) * e_lev - rho)
        here, _, _, _, rate = plain(0)
        store(0, g, h, begin, here, rate - div)
        store(4, g, h, begin, e, e_rate - GAMMA_HEAT * div)

    def section(s, x, store):
        first_half = jnp.where(low_a, 1, 0)

        def block(i, carry):
            second = jnp.where(lat_edge, i // 2, i % 2)
            cols_part = jnp.where(lat_edge, i % 2, i // 2)
            h = jnp.where(second == 0, first_half, 1 - first_half)

            @pl.when(cols_part == 0)
            def _():
                wait_rows(s, x, h)

            @pl.when(jnp.logical_and(cols_part == 1, second == 0))
            def _():
                wait_cols(s, x)

            def step(k, inside):
                for one in range(2):
                    g = jnp.where(cols_part == 0, 2 + 2 * k + one, 1 + (GROUPS - 1) * one)
                    group_rates(x, g, h, store)
                return inside

            lax.fori_loop(0, jnp.where(cols_part == 0, (GROUPS - 2) // 2, 1), step, 0)
            if s == 0:

                @pl.when(cols_part == 1)
                def _():
                    send_half(1, x2, h)

            return carry

        lax.fori_loop(0, 4, block, 0)

    def store_first(f, g, h, begin, here, rate):
        x2[f, g, pl.ds(pl.multiple_of(TOP + 8 * h, 8), 8), :] = here + TIME_STEP * rate

    def store_second(f, g, h, begin, here, rate):
        before = x1[f, g, pl.ds(pl.multiple_of(TOP + 8 * h, 8), 8), :]
        out[0, f, pl.ds(pl.multiple_of(8 * h, 8), 8), pl.ds(begin, LANES)] = 0.5 * (
            before + here + TIME_STEP * rate
        )

    section(0, x1, store_first)
    export(1, x2)
    for copy in rim_copies(1):
        copy.start()
    section(1, x2, store_second)

    for s, x in enumerate((x1, x2)):
        for copy in rim_copies(s):
            copy.wait_send()
        for h in range(2):
            for there, copy in [row_copy(s, x, h)] + col_copies(s, x, h):

                @pl.when(there)
                def _():
                    copy.wait_send()


def on_device(*operands):
    n_lat = lax.axis_size("lat")
    n_lon = lax.axis_size("lon")
    operands = list(operands)
    operands[2] = operands[2].reshape(LAT_BLOCK, 1, LANES)
    operands[3] = operands[3].reshape(LON_BLOCK, 1, LANES)
    operands = [pltpu.with_memory_space_constraint(x, pltpu.HBM) for x in operands]

    def body(*refs):
        kernel(n_lat, n_lon, *refs)

    def vmem(*shape):
        return pltpu.VMEM(shape, jnp.float32)

    return pl.pallas_call(
        body,
        out_shape=jax.ShapeDtypeStruct(operands[0].shape, jnp.float32),
        in_specs=[pl.BlockSpec(memory_space=pltpu.HBM)] * 10,
        out_specs=pl.BlockSpec(memory_space=pltpu.VMEM),
        scratch_shapes=[
            vmem(FIELDS, GROUPS + 2, 32, LANES),
            vmem(FIELDS, GROUPS + 2, 32, LANES),
            vmem(1, CLAT, GROUPS * LANES),
            vmem(LAT_BLOCK, 1, LANES),
            vmem(LON_BLOCK, 1, LANES),
            pltpu.SMEM((1, 1, 1, LAT_BLOCK), jnp.float32),
            pltpu.SMEM((1, 1, 1, LON_BLOCK), jnp.float32),
            pltpu.SMEM((1, 1, 1, 2), jnp.int32),
            pltpu.SMEM((1, 1, 1, 2), jnp.int32),
            pltpu.VMEM((2, 1, n_lat), jnp.int32),
            pltpu.VMEM((2, 1, n_lon), jnp.int32),
            vmem(32, 2 * LANES),
            pltpu.VMEM((2, LANES, GROUPS * CLAT), jnp.bfloat16),
            vmem(2, 2, 8, LANES),
            vmem(2, BLOCK_ROWS, LANES),
            vmem(2, 2, 8, LANES),
            vmem(2 * n_lat * BLOCK_ROWS, LANES),
            vmem(2 * n_lon * 8, LANES),
            pltpu.SemaphoreType.DMA((10,)),
            pltpu.SemaphoreType.DMA((2, 3, 2)),
            pltpu.SemaphoreType.DMA((2, 3, 2)),
            pltpu.SemaphoreType.DMA((2, 4)),
            pltpu.SemaphoreType.DMA((2, 2)),
        ],
        compiler_params=pltpu.CompilerParams(
            collective_id=0, has_side_effects=True, vmem_limit_bytes=40 * 1024 * 1024
        ),
    )(*operands)


def solution(mesh):
    in_specs = (
        P("yy", None, "lat", "lon"),
        P("yy", "lat", "lon"),
        P("yy", "lat", "lon", None, None),
        P("yy", "lat", "lon", None, None),
        P("yy", "lat", "lon", None),
        P("yy", "lat", "lon", None),
        P("yy", "lat", "lon", None),
        P("yy", "lat", "lon", None),
        P(None, "lon", None),
        P(None, "lat", None),
    )
    out_specs = P("yy", None, "lat", "lon")
    return jax.shard_map(
        on_device, mesh=mesh, in_specs=in_specs, out_specs=out_specs, check_vma=False
    )
```

```python
import math

import jax
import jax.numpy as jnp
from jax import lax
from jax.experimental import pallas as pl
from jax.experimental.pallas import tpu as pltpu
from jax.sharding import PartitionSpec as P

FIELDS = 5
LEV = 32
CLAT = 16
GROUPS = 18
LANES = 128
PATCH_H = 8
PATCH_W = 16
LAT_BLOCK = 18
LON_BLOCK = 6
SPAN = 5
BLOCK_ROWS = 32
TOP = 8

TIME_STEP = 0.2
KAPPA_PRESS = 0.4
GAMMA_HEAT = 1.4

MESH = pl.DeviceIdType.MESH


def dot(left, right):
    return jnp.dot(left, right, preferred_element_type=jnp.float32)


def iota(shape, axis):
    return lax.broadcasted_iota(jnp.int32, shape, axis)


def split(value, parts):
    pieces = []
    for _ in range(parts):
        piece = value.astype(jnp.bfloat16)
        pieces.append(piece)
        value = value - piece.astype(jnp.float32)
    return pieces


def kernel(
    n_lat,
    n_lon,
    fields_hbm,
    visc_hbm,
    lat_w_hbm,
    lon_w_hbm,
    lat_ang_hbm,
    lon_ang_hbm,
    rows_hbm,
    cols_hbm,
    lat_pair_hbm,
    lon_pair_hbm,
    out,
    x1,
    x2,
    hz,
    visc,
    lat_w,
    lon_w,
    lat_ang,
    lon_ang,
    rows,
    cols,
    lat_pair,
    lon_pair,
    wp,
    mat,
    metric,
    zbuf,
    wbuf,
    rl,
    rw,
    local,
    halo_send,
    halo_recv,
    rim_send,
    rim_recv,
):
    p = lax.axis_index("yy")
    a = lax.axis_index("lat")
    b = lax.axis_index("lon")
    q = 1 - p
    low_a, high_a = a == 0, a == n_lat - 1
    low_b, high_b = b == 0, b == n_lon - 1
    lat_edge = jnp.logical_or(low_a, high_a)
    lon_edge = jnp.logical_or(low_b, high_b)
    neighbours = (
        (jnp.logical_not(low_a), (p, a - 1, b)),
        (jnp.logical_not(high_a), (p, a + 1, b)),
        (jnp.logical_not(low_b), (p, a, b - 1)),
        (jnp.logical_not(high_b), (p, a, b + 1)),
    )

    barrier = pltpu.get_barrier_semaphore()
    for there, device in neighbours:

        @pl.when(there)
        def _():
            pl.semaphore_signal(barrier, inc=1, device_id=device, device_id_type=MESH)

    @pl.when(lat_edge)
    def _():
        def one(i, carry):
            pl.semaphore_signal(barrier, inc=1, device_id=(q, i, b), device_id_type=MESH)
            return carry

        lax.fori_loop(0, n_lat, one, 0)

    @pl.when(lon_edge)
    def _():
        def one(i, carry):
            pl.semaphore_signal(barrier, inc=1, device_id=(q, a, i), device_id_type=MESH)
            return carry

        lax.fori_loop(0, n_lon, one, 0)

    small = [
        pltpu.make_async_copy(src, dst, local.at[i])
        for i, (src, dst) in enumerate(
            (
                (lat_w_hbm, lat_w),
                (lon_w_hbm, lon_w),
                (lat_ang_hbm, lat_ang),
                (lon_ang_hbm, lon_ang),
                (rows_hbm, rows),
                (cols_hbm, cols),
                (lat_pair_hbm, lat_pair),
                (lon_pair_hbm, lon_pair),
                (visc_hbm, visc),
            )
        )
    ]
    for copy in small[:6]:
        copy.start()
    inner = pl.ds(1, GROUPS)
    for g in range(GROUPS):
        pltpu.make_async_copy(
            fields_hbm.at[0, :, :, pl.ds(g * LANES, LANES)],
            x1.at[:, g + 1, pl.ds(TOP, CLAT), :],
            local.at[9],
        ).start()
    for copy in small[6:]:
        copy.start()

    wp[...] = jnp.zeros_like(wp)
    for copy in small[:6]:
        copy.wait()
    for t in range(LAT_BLOCK):
        u, v = t // 4, t % 4
        wp[v * 8 + u : v * 8 + u + 1, 0:LANES] = lat_w[t]
    for t in range(LON_BLOCK):
        u, v = (5, t + 1) if t < 3 else (6, t - 3)
        wp[v * 8 + u : v * 8 + u + 1, LANES : 2 * LANES] = lon_w[t]
    weights = jnp.concatenate(split(wp[...], 3), axis=0)
    entry = iota((2 * LANES, GROUPS * CLAT), 0)
    place = iota((2 * LANES, GROUPS * CLAT), 1)
    is_lon = entry >= LANES
    entry = entry & (LANES - 1)
    row0 = jnp.where(is_lon, rows[0, 0, 0, 1], rows[0, 0, 0, 0])
    col0 = jnp.where(is_lon, cols[0, 0, 0, 1], cols[0, 0, 0, 0])
    from_col = (entry & (PATCH_W - 1)) - 4 * (place >> 4) + col0
    same_row = (place & (CLAT - 1)) - (entry >> 4) == row0
    from_col = jnp.where(same_row, from_col, -1)
    for kk in range(4):
        chosen = jnp.where(from_col == kk, 1.0, 0.0).astype(jnp.bfloat16)
        parts = dot(weights, chosen)
        part = parts[0:32] + parts[32:64] + parts[64:96]
        high, low = split(part, 2)
        mat[0, kk * 32 : (kk + 1) * 32, :] = high
        mat[1, kk * 32 : (kk + 1) * 32, :] = low

    lane = iota((8, LANES), 1)
    sub = iota((8, LANES), 0)
    lane_group = lane >> 5
    target = 4 * sub + lane_group
    angle = jnp.zeros((8, LANES), jnp.float32)
    for t in range(LAT_BLOCK):
        angle = jnp.where(target == t, lat_ang[0, 0, 0, t], angle)
    for t in range(LON_BLOCK):
        u, v = (5, t + 1) if t < 3 else (6, t - 3)
        angle = jnp.where(target == 4 * u + v, lon_ang[0, 0, 0, t], angle)
    cos_angle = jnp.cos(angle)
    sin_angle = jnp.sin(angle)

    def export(s, x):
        columns = []
        for f in range(FIELDS):
            columns.append(x[f, 1 : GROUPS + 1, TOP : TOP + CLAT, :].reshape(GROUPS * CLAT, LANES))
        high, low = split(jnp.concatenate(columns, axis=1), 2)
        total = dot(mat[0], high) + dot(mat[0], low) + dot(mat[1], high)
        blocks = []
        for f in range(FIELDS):
            piece = total[:, f * LANES : (f + 1) * LANES]
            result = None
            for shift in range(4):
                mixed = None
                for kk in range(4):
                    v = (kk + shift) % 4
                    part = piece[kk * 32 + v * 8 : kk * 32 + v * 8 + 8, :]
                    mixed = part if mixed is None else jnp.where(lane_group == kk, part, mixed)
                if shift:
                    mixed = pltpu.roll(mixed, 32 * shift, 1)
                result = mixed if result is None else result + mixed
            blocks.append(result)
        east = cos_angle * blocks[1] + sin_angle * blocks[2]
        north = cos_angle * blocks[2] - sin_angle * blocks[1]
        blocks[1], blocks[2] = east, north
        for f in range(FIELDS):
            zbuf[s, SPAN * f : SPAN * f + SPAN, :] = blocks[f][0:SPAN]
            wbuf[s, 0, f : f + 1, :] = blocks[f][5:6]
            wbuf[s, 1, f : f + 1, :] = blocks[f][6:7]

    def rim_copies(s):
        lat_dst = rl.at[pl.ds((s * n_lat + a) * BLOCK_ROWS, BLOCK_ROWS), :]
        lon_dst = rw.at[pl.ds((s * n_lon + b) * 8, 8), :]
        ends = (
            (zbuf.at[s], lat_dst, (q, 0, b), 0),
            (zbuf.at[s], lat_dst, (q, n_lat - 1, b), 0),
            (wbuf.at[s, 0], lon_dst, (q, a, 0), 1),
            (wbuf.at[s, 1], lon_dst, (q, a, n_lon - 1), 1),
        )
        return [
            pltpu.make_async_remote_copy(
                src_ref=src,
                dst_ref=dst,
                send_sem=rim_send.at[s, i],
                recv_sem=rim_recv.at[s, kind],
                device_id=device,
                device_id_type=MESH,
            )
            for i, (src, dst, device, kind) in enumerate(ends)
        ]

    def row_copy(s, x, h):
        there = jnp.where(h == 0, jnp.logical_not(low_a), jnp.logical_not(high_a))
        return there, pltpu.make_async_remote_copy(
            src_ref=x.at[:, inner, pl.ds(TOP + (CLAT - 3) * h, 3), :],
            dst_ref=hz.at[s, 1 - h, :, :, pl.ds(8 - 3 * h, 3), :],
            send_sem=halo_send.at[s, 0, h],
            recv_sem=halo_recv.at[s, 0, h],
            device_id=(p, a + 2 * h - 1, b),
            device_id_type=MESH,
        )

    def col_copies(s, x, h):
        band = pl.ds(pl.multiple_of(TOP + 8 * h, 8), 8)
        ends = ((1, GROUPS + 1), (GROUPS, 0))
        return [
            (
                neighbours[2 + i][0],
                pltpu.make_async_remote_copy(
                    src_ref=x.at[:, src, band, :],
                    dst_ref=x.at[:, dst, band, :],
                    send_sem=halo_send.at[s, 1 + i, h],
                    recv_sem=halo_recv.at[s, 1 + i, h],
                    device_id=neighbours[2 + i][1],
                    device_id_type=MESH,
                ),
            )
            for i, (src, dst) in enumerate(ends)
        ]

    def send_half(s, x, h):
        for there, copy in [row_copy(s, x, h)] + col_copies(s, x, h):

            @pl.when(there)
            def _():
                copy.start()

    pltpu.make_async_copy(
        x1.at[:, inner, pl.ds(TOP, CLAT), :], x1.at[:, inner, pl.ds(TOP, CLAT), :], local.at[9]
    ).wait()
    export(0, x1)

    count = 4
    for there, _ in neighbours:
        count = count + jnp.where(there, 1, 0)
    pl.semaphore_wait(barrier, count)

    for copy in rim_copies(0):
        copy.start()
    for h in range(2):
        send_half(0, x1, h)

    none = jnp.zeros((8, LANES), jnp.float32)

    def clear(g, carry):
        for f in range(FIELDS):
            for s, x in enumerate((x1, x2)):
                x[f, g + 1, TOP - 8 : TOP, :] = none
                x[f, g + 1, TOP + CLAT : TOP + CLAT + 8, :] = none
                hz[s, 0, f, g, 8:16, :] = none
                hz[s, 1, f, g, 0:8, :] = none
        return carry

    lax.fori_loop(0, GROUPS, clear, 0)

    for copy in small[6:]:
        copy.wait()
    total_rows = CLAT * n_lat
    for h in range(2):
        row = (a * CLAT + 8 * h + sub).astype(jnp.float32)
        cosine = jnp.cos((row + 0.5 - 0.5 * total_rows) * (0.5 * math.pi / total_rows))
        metric[h, 0] = 1.0 / (60.0 * cosine)
        metric[h, 1] = 1.0 / (cosine * cosine)

    k_lat = (
        4 * (iota((32, n_lat), 0) & 7)
        + (iota((32, n_lat), 0) >> 3)
        + jnp.where(low_a, 0, n_lat // 2)
    )
    choose_lat = jnp.where(lat_pair[p] == k_lat, 1.0, 0.0).astype(jnp.bfloat16)
    choose_lon = jnp.where(lon_pair[p] == iota((CLAT, n_lon), 0), 1.0, 0.0).astype(jnp.bfloat16)

    def place_lat(s, side, first_row):
        half = lane < 64
        for f in range(FIELDS):
            got = jnp.concatenate(
                [
                    rl[pl.ds(s * n_lat * BLOCK_ROWS + SPAN * f + u, n_lat, stride=BLOCK_ROWS), :]
                    for u in range(SPAN)
                ],
                axis=1,
            )
            placed = None
            for piece in split(got, 3):
                term = dot(choose_lat, piece)
                placed = term if placed is None else placed + term
            for c in range(2):
                plain = [placed[16 * c : 16 * c + 8, u * LANES : (u + 1) * LANES] for u in range(SPAN)]
                moved = [
                    pltpu.roll(placed[16 * c + 8 : 16 * c + 16, u * LANES : (u + 1) * LANES], 64, 1)
                    for u in range(SPAN)
                ]
                tiles = plain[:4] + [jnp.where(half, plain[4], moved[0])]
                tiles += [jnp.where(half, moved[u], moved[u + 1]) for u in range(4)]
                for g, value in enumerate(tiles):
                    hz[s, side, f, 9 * c + g, first_row : first_row + 3, :] = value[0:3]

    def place_lon(s, x, group):
        got = jnp.concatenate(
            [rw[pl.ds(s * n_lon * 8 + f, n_lon, stride=8), :] for f in range(FIELDS)], axis=1
        )
        placed = None
        for piece in split(got, 3):
            term = dot(choose_lon, piece)
            placed = term if placed is None else placed + term
        for f in range(FIELDS):
            x[f, group, TOP : TOP + CLAT, :] = placed[:, f * LANES : (f + 1) * LANES]

    def wait_rows(s, h):
        there = jnp.where(h == 0, jnp.logical_not(low_a), jnp.logical_not(high_a))

        @pl.when(there)
        def _():
            row_copy(s, x1, 1 - h)[1].wait_recv()

        @pl.when(jnp.logical_not(there))
        def _():
            got = rl.at[pl.ds(s * n_lat * BLOCK_ROWS, n_lat * BLOCK_ROWS), :]
            pltpu.make_async_copy(got, got, rim_recv.at[s, 0]).wait()

        @pl.when(jnp.logical_and(h == 0, low_a))
        def _():
            place_lat(s, 0, 5)

        @pl.when(jnp.logical_and(h == 1, high_a))
        def _():
            place_lat(s, 1, 8)

    def wait_cols(s, x):
        for h in range(2):
            (west, to_west), (east, to_east) = col_copies(s, x, h)

            @pl.when(west)
            def _():
                to_east.wait_recv()

            @pl.when(east)
            def _():
                to_west.wait_recv()

        @pl.when(lon_edge)
        def _():
            got = rw.at[pl.ds(s * n_lon * 8, n_lon * 8), :]
            pltpu.make_async_copy(got, got, rim_recv.at[s, 1]).wait()

        @pl.when(low_b)
        def _():
            place_lon(s, x, 0)

        @pl.when(high_b)
        def _():
            place_lon(s, x, GROUPS + 1)

    not_last = (lane & (LEV - 1)) != LEV - 1
    not_first = (lane & (LEV - 1)) != 0

    def derivatives(x, f, g, r):
        def row(o):
            return x[f, g, pl.ds(r + o, 8), :]

        here = row(0)
        west, east = x[f, g - 1, pl.ds(r, 8), :], x[f, g + 1, pl.ds(r, 8), :]
        up1, down1 = row(1), row(-1)
        lat = (
            0.75 * (up1 - down1) - 0.15 * (row(2) - row(-2)) + (1.0 / 60.0) * (row(3) - row(-3))
        )
        plus1 = pltpu.roll(jnp.where(lane < 32, east, here), 96, 1)
        minus1 = pltpu.roll(jnp.where(lane >= 96, west, here), 32, 1)
        two = pltpu.roll(jnp.where(lane < 64, east - here, here - west), 64, 1)
        plus3 = pltpu.roll(jnp.where(lane < 96, east, here), 32, 1)
        minus3 = pltpu.roll(jnp.where(lane >= 32, west, here), 96, 1)
        lon = 45.0 * (plus1 - minus1) - 9.0 * two + (plus3 - minus3)
        upper = jnp.where(not_last, pltpu.roll(here, LANES - 1, 1), 0.0)
        lower = jnp.where(not_first, pltpu.roll(here, 1, 1), 0.0)
        return here, lat, lon, upper - lower, up1 + down1, plus1 + minus1

    def group_rates(x, g, h, store):
        r = pl.multiple_of(TOP + 8 * h, 8)
        begin = pl.multiple_of((g - 1) * LANES, LANES)
        inv_lon, inv_sq = metric[h, 0], metric[h, 1]
        centre = 2.0 + 2.0 * inv_sq
        u = x[1, g, pl.ds(r, 8), :] * inv_lon
        v = x[2, g, pl.ds(r, 8), :]
        w = x[3, g, pl.ds(r, 8), :] * 0.5
        rho = x[0, g, pl.ds(r, 8), :]
        nu = visc[0, pl.ds(pl.multiple_of(8 * h, 8), 8), pl.ds(begin, LANES)]

        def plain(f):
            here, lat, lon, lev, rows_sum, cols_sum = derivatives(x, f, g, r)
            lap = rows_sum + cols_sum * inv_sq - centre * here
            return here, lat, lon, lev, nu * lap - (u * lon + v * lat + w * lev)

        e, e_lat, e_lon, e_lev, e_rate = plain(4)
        here, _, lon, _, rate = plain(1)
        div = lon * inv_lon
        store(1, g, h, begin, here, rate - KAPPA_PRESS * (e_lon * inv_lon))
        here, lat, _, _, rate = plain(2)
        div = div + lat
        store(2, g, h, begin, here, rate - KAPPA_PRESS * e_lat)
        here, _, _, lev, rate = plain(3)
        div = div + 0.5 * lev
        store(3, g, h, begin, here, rate - (0.5 * KAPPA_PRESS) * e_lev - rho)
        here, _, _, _, rate = plain(0)
        store(0, g, h, begin, here, rate - div)
        store(4, g, h, begin, e, e_rate - GAMMA_HEAT * div)

    def correct(s, x, h, add):
        r = pl.multiple_of(TOP + 8 * h, 8)
        sign = jnp.where(h == 0, -1.0, 1.0)

        def step(k, carry):
            for one in range(2):
                g = 1 + 2 * k + one
                begin = pl.multiple_of((g - 1) * LANES, LANES)
                v = x[2, g, pl.ds(r, 8), :]
                nu = visc[0, pl.ds(pl.multiple_of(8 * h, 8), 8), pl.ds(begin, LANES)]

                def share(f):
                    near, middle, far = (
                        hz[s, h, f, g - 1, pl.ds(jnp.where(h == 0, 8 - o, o), 8), :]
                        for o in (1, 2, 3)
                    )
                    lat = sign * (0.75 * near - 0.15 * middle + (1.0 / 60.0) * far)
                    return lat, nu * near - v * lat

                e_lat, e_rate = share(4)
                v_lat, v_rate = share(2)
                add(2, g, h, begin, v_rate - KAPPA_PRESS * e_lat)
                add(4, g, h, begin, e_rate - GAMMA_HEAT * v_lat)
                add(0, g, h, begin, share(0)[1] - v_lat)
                add(1, g, h, begin, share(1)[1])
                add(3, g, h, begin, share(3)[1])
            return carry

        lax.fori_loop(0, GROUPS // 2, step, 0)

    def section(s, x, store, add):
        def block(i, carry):
            @pl.when(i == 1)
            def _():
                wait_cols(s, x)

            def step(k, inside):
                for one in range(2):
                    g = jnp.where(i == 0, 2 + 2 * (k // 2) + one, 1 + (GROUPS - 1) * one)
                    group_rates(x, g, k % 2, store)
                return inside

            lax.fori_loop(0, jnp.where(i == 0, GROUPS - 2, 2), step, 0)
            return carry

        lax.fori_loop(0, 2, block, 0)

        def side(i, carry):
            h = jnp.where(low_a, 1 - i, i)
            wait_rows(s, h)
            correct(s, x, h, add)
            if s == 0:
                send_half(1, x2, h)
            return carry

        lax.fori_loop(0, 2, side, 0)

    def store_first(f, g, h, begin, here, rate):
        x2[f, g, pl.ds(pl.multiple_of(TOP + 8 * h, 8), 8), :] = here + TIME_STEP * rate

    def store_second(f, g, h, begin, here, rate):
        before = x1[f, g, pl.ds(pl.multiple_of(TOP + 8 * h, 8), 8), :]
        out[0, f, pl.ds(pl.multiple_of(8 * h, 8), 8), pl.ds(begin, LANES)] = 0.5 * (
            before + here + TIME_STEP * rate
        )

    def add_first(f, g, h, begin, rate):
        x2[f, g, pl.ds(pl.multiple_of(TOP + 8 * h, 8), 8), :] += TIME_STEP * rate

    def add_second(f, g, h, begin, rate):
        out[0, f, pl.ds(pl.multiple_of(8 * h, 8), 8), pl.ds(begin, LANES)] += (
            0.5 * TIME_STEP * rate
        )

    section(0, x1, store_first, add_first)
    export(1, x2)
    for copy in rim_copies(1):
        copy.start()
    section(1, x2, store_second, add_second)

    for s, x in enumerate((x1, x2)):
        for copy in rim_copies(s):
            copy.wait_send()
        for h in range(2):
            for there, copy in [row_copy(s, x, h)] + col_copies(s, x, h):

                @pl.when(there)
                def _():
                    copy.wait_send()


def on_device(*operands):
    n_lat = lax.axis_size("lat")
    n_lon = lax.axis_size("lon")
    operands = list(operands)
    operands[2] = operands[2].reshape(LAT_BLOCK, 1, LANES)
    operands[3] = operands[3].reshape(LON_BLOCK, 1, LANES)
    operands = [pltpu.with_memory_space_constraint(x, pltpu.HBM) for x in operands]

    def body(*refs):
        kernel(n_lat, n_lon, *refs)

    def vmem(*shape):
        return pltpu.VMEM(shape, jnp.float32)

    return pl.pallas_call(
        body,
        out_shape=jax.ShapeDtypeStruct(operands[0].shape, jnp.float32),
        in_specs=[pl.BlockSpec(memory_space=pltpu.HBM)] * 10,
        out_specs=pl.BlockSpec(memory_space=pltpu.VMEM),
        scratch_shapes=[
            vmem(FIELDS, GROUPS + 2, 32, LANES),
            vmem(FIELDS, GROUPS + 2, 32, LANES),
            vmem(2, 2, FIELDS, GROUPS, 16, LANES),
            vmem(1, CLAT, GROUPS * LANES),
            vmem(LAT_BLOCK, 1, LANES),
            vmem(LON_BLOCK, 1, LANES),
            pltpu.SMEM((1, 1, 1, LAT_BLOCK), jnp.float32),
            pltpu.SMEM((1, 1, 1, LON_BLOCK), jnp.float32),
            pltpu.SMEM((1, 1, 1, 2), jnp.int32),
            pltpu.SMEM((1, 1, 1, 2), jnp.int32),
            pltpu.VMEM((2, 1, n_lat), jnp.int32),
            pltpu.VMEM((2, 1, n_lon), jnp.int32),
            vmem(32, 2 * LANES),
            pltpu.VMEM((2, LANES, GROUPS * CLAT), jnp.bfloat16),
            vmem(2, 2, 8, LANES),
            vmem(2, BLOCK_ROWS, LANES),
            vmem(2, 2, 8, LANES),
            vmem(2 * n_lat * BLOCK_ROWS, LANES),
            vmem(2 * n_lon * 8, LANES),
            pltpu.SemaphoreType.DMA((10,)),
            pltpu.SemaphoreType.DMA((2, 3, 2)),
            pltpu.SemaphoreType.DMA((2, 3, 2)),
            pltpu.SemaphoreType.DMA((2, 4)),
            pltpu.SemaphoreType.DMA((2, 2)),
        ],
        compiler_params=pltpu.CompilerParams(
            collective_id=0, has_side_effects=True, vmem_limit_bytes=40 * 1024 * 1024
        ),
    )(*operands)


def solution(mesh):
    in_specs = (
        P("yy", None, "lat", "lon"),
        P("yy", "lat", "lon"),
        P("yy", "lat", "lon", None, None),
        P("yy", "lat", "lon", None, None),
        P("yy", "lat", "lon", None),
        P("yy", "lat", "lon", None),
        P("yy", "lat", "lon", None),
        P("yy", "lat", "lon", None),
        P(None, "lon", None),
        P(None, "lat", None),
    )
    out_specs = P("yy", None, "lat", "lon")
    return jax.shard_map(
        on_device, mesh=mesh, in_specs=in_specs, out_specs=out_specs, check_vma=False
    )
```

```python
import math

import jax
import jax.numpy as jnp
from jax import lax
from jax.experimental import pallas as pl
from jax.experimental.pallas import tpu as pltpu
from jax.sharding import PartitionSpec as P

FIELDS = 5
LEV = 32
CLAT = 16
GROUPS = 18
LANES = 128
PATCH_H = 8
PATCH_W = 16
LAT_BLOCK = 18
LON_BLOCK = 6
SPAN = 5
BLOCK_ROWS = 23
WIDE_ROWS = 5
TOP = 8

TIME_STEP = 0.2
KAPPA_PRESS = 0.4
GAMMA_HEAT = 1.4

MESH = pl.DeviceIdType.MESH


def dot(left, right):
    return jnp.dot(left, right, preferred_element_type=jnp.float32)


def iota(shape, axis):
    return lax.broadcasted_iota(jnp.int32, shape, axis)


def split(value, parts):
    pieces = []
    for _ in range(parts):
        piece = value.astype(jnp.bfloat16)
        pieces.append(piece)
        value = value - piece.astype(jnp.float32)
    return pieces


def kernel(
    n_lat,
    n_lon,
    fields_hbm,
    visc_hbm,
    lat_w_hbm,
    lon_w_hbm,
    lat_ang_hbm,
    lon_ang_hbm,
    rows_hbm,
    cols_hbm,
    lat_pair_hbm,
    lon_pair_hbm,
    out,
    x1,
    x2,
    hz,
    visc,
    lat_w,
    lon_w,
    lat_ang,
    lon_ang,
    rows,
    cols,
    lat_pair,
    lon_pair,
    wp,
    mat,
    metric,
    zbuf,
    wbuf,
    rl,
    rw,
    local,
    halo_send,
    halo_recv,
    rim_send,
    rim_recv,
):
    p = lax.axis_index("yy")
    a = lax.axis_index("lat")
    b = lax.axis_index("lon")
    q = 1 - p
    low_a, high_a = a == 0, a == n_lat - 1
    low_b, high_b = b == 0, b == n_lon - 1
    lat_edge = jnp.logical_or(low_a, high_a)
    lon_edge = jnp.logical_or(low_b, high_b)
    neighbours = (
        (jnp.logical_not(low_a), (p, a - 1, b)),
        (jnp.logical_not(high_a), (p, a + 1, b)),
        (jnp.logical_not(low_b), (p, a, b - 1)),
        (jnp.logical_not(high_b), (p, a, b + 1)),
    )

    barrier = pltpu.get_barrier_semaphore()
    for there, device in neighbours:

        @pl.when(there)
        def _():
            pl.semaphore_signal(barrier, inc=1, device_id=device, device_id_type=MESH)

    @pl.when(lat_edge)
    def _():
        ring = n_lat // 2

        def one(k, carry):
            away = ring // 2 + jnp.where(k % 2 == 1, -((k + 1) // 2), k // 2)
            for part in range(2):
                there = part * ring + lax.rem(a + away, ring)
                pl.semaphore_signal(
                    barrier, inc=1, device_id=(q, there, b), device_id_type=MESH
                )
            return carry

        lax.fori_loop(0, ring, one, 0)

    @pl.when(lon_edge)
    def _():
        def one(i, carry):
            pl.semaphore_signal(barrier, inc=1, device_id=(q, a, i), device_id_type=MESH)
            return carry

        lax.fori_loop(0, n_lon, one, 0)

    small = [
        pltpu.make_async_copy(src, dst, local.at[i])
        for i, (src, dst) in enumerate(
            (
                (lat_w_hbm, lat_w),
                (lon_w_hbm, lon_w),
                (lat_ang_hbm, lat_ang),
                (lon_ang_hbm, lon_ang),
                (rows_hbm, rows),
                (cols_hbm, cols),
                (lat_pair_hbm, lat_pair),
                (lon_pair_hbm, lon_pair),
                (visc_hbm, visc),
            )
        )
    ]
    for copy in small[:6]:
        copy.start()
    inner = pl.ds(1, GROUPS)
    for g in range(GROUPS):
        pltpu.make_async_copy(
            fields_hbm.at[0, :, :, pl.ds(g * LANES, LANES)],
            x1.at[:, g + 1, pl.ds(TOP, CLAT), :],
            local.at[9],
        ).start()
    for copy in small[6:]:
        copy.start()

    wp[...] = jnp.zeros_like(wp)
    for copy in small[:6]:
        copy.wait()
    for t in range(LAT_BLOCK):
        u, v = t // 4, t % 4
        wp[v * 8 + u : v * 8 + u + 1, 0:LANES] = lat_w[t]
    for t in range(LON_BLOCK):
        u, v = (5, t + 1) if t < 3 else (6, t - 3)
        wp[v * 8 + u : v * 8 + u + 1, LANES : 2 * LANES] = lon_w[t]
    weights = jnp.concatenate(split(wp[...], 3), axis=0)
    entry = iota((2 * LANES, GROUPS * CLAT), 0)
    place = iota((2 * LANES, GROUPS * CLAT), 1)
    is_lon = entry >= LANES
    entry = entry & (LANES - 1)
    row0 = jnp.where(is_lon, rows[0, 0, 0, 1], rows[0, 0, 0, 0])
    col0 = jnp.where(is_lon, cols[0, 0, 0, 1], cols[0, 0, 0, 0])
    from_col = (entry & (PATCH_W - 1)) - 4 * (place >> 4) + col0
    same_row = (place & (CLAT - 1)) - (entry >> 4) == row0
    from_col = jnp.where(same_row, from_col, -1)
    for kk in range(4):
        chosen = jnp.where(from_col == kk, 1.0, 0.0).astype(jnp.bfloat16)
        parts = dot(weights, chosen)
        part = parts[0:32] + parts[32:64] + parts[64:96]
        high, low = split(part, 2)
        mat[0, kk * 32 : (kk + 1) * 32, :] = high
        mat[1, kk * 32 : (kk + 1) * 32, :] = low

    lane = iota((8, LANES), 1)
    sub = iota((8, LANES), 0)
    lane_group = lane >> 5
    target = 4 * sub + lane_group
    angle = jnp.zeros((8, LANES), jnp.float32)
    for t in range(LAT_BLOCK):
        angle = jnp.where(target == t, lat_ang[0, 0, 0, t], angle)
    for t in range(LON_BLOCK):
        u, v = (5, t + 1) if t < 3 else (6, t - 3)
        angle = jnp.where(target == 4 * u + v, lon_ang[0, 0, 0, t], angle)
    cos_angle = jnp.cos(angle)
    sin_angle = jnp.sin(angle)

    def export(s, x):
        columns = []
        for f in range(FIELDS):
            columns.append(x[f, 1 : GROUPS + 1, TOP : TOP + CLAT, :].reshape(GROUPS * CLAT, LANES))
        high, low = split(jnp.concatenate(columns, axis=1), 2)
        total = dot(mat[0], high) + dot(mat[0], low) + dot(mat[1], high)
        blocks = []
        for f in range(FIELDS):
            piece = total[:, f * LANES : (f + 1) * LANES]
            result = None
            for shift in range(4):
                mixed = None
                for kk in range(4):
                    v = (kk + shift) % 4
                    part = piece[kk * 32 + v * 8 : kk * 32 + v * 8 + 8, :]
                    mixed = part if mixed is None else jnp.where(lane_group == kk, part, mixed)
                if shift:
                    mixed = pltpu.roll(mixed, 32 * shift, 1)
                result = mixed if result is None else result + mixed
            blocks.append(result)
        east = cos_angle * blocks[1] + sin_angle * blocks[2]
        north = cos_angle * blocks[2] - sin_angle * blocks[1]
        blocks[1], blocks[2] = east, north
        for f in range(FIELDS):
            zbuf[s, 4 * f : 4 * f + 4, :] = blocks[f][0:4]
            last = blocks[f][4:5]
            if f % 2 == 0 and f + 1 < FIELDS:
                last = jnp.where(
                    lane[0:1] < 64, last, pltpu.roll(blocks[f + 1], 64, 1)[4:5]
                )
            if f % 2 == 0:
                zbuf[s, 4 * FIELDS + f // 2 : 4 * FIELDS + f // 2 + 1, :] = last
            wbuf[s, 0, f : f + 1, :] = blocks[f][5:6]
            wbuf[s, 1, f : f + 1, :] = blocks[f][6:7]

    def rim_copies(s):
        lat_dst = rl.at[pl.ds((s * n_lat + a) * BLOCK_ROWS, BLOCK_ROWS), :]
        lon_dst = rw.at[pl.ds((s * n_lon + b) * WIDE_ROWS, WIDE_ROWS), :]
        ends = (
            (zbuf.at[s], lat_dst, (q, 0, b), 0),
            (zbuf.at[s], lat_dst, (q, n_lat - 1, b), 0),
            (wbuf.at[s, 0], lon_dst, (q, a, 0), 1),
            (wbuf.at[s, 1], lon_dst, (q, a, n_lon - 1), 1),
        )
        return [
            pltpu.make_async_remote_copy(
                src_ref=src,
                dst_ref=dst,
                send_sem=rim_send.at[s, i],
                recv_sem=rim_recv.at[s, kind],
                device_id=device,
                device_id_type=MESH,
            )
            for i, (src, dst, device, kind) in enumerate(ends)
        ]

    def row_copy(s, x, h):
        there = jnp.where(h == 0, jnp.logical_not(low_a), jnp.logical_not(high_a))
        return there, pltpu.make_async_remote_copy(
            src_ref=x.at[:, inner, pl.ds(TOP + (CLAT - 3) * h, 3), :],
            dst_ref=hz.at[s, 1 - h, :, :, pl.ds(8 - 3 * h, 3), :],
            send_sem=halo_send.at[s, 0, h],
            recv_sem=halo_recv.at[s, 0, h],
            device_id=(p, a + 2 * h - 1, b),
            device_id_type=MESH,
        )

    def col_copies(s, x, h):
        band = pl.ds(pl.multiple_of(TOP + 8 * h, 8), 8)
        ends = ((1, GROUPS + 1), (GROUPS, 0))
        return [
            (
                neighbours[2 + i][0],
                pltpu.make_async_remote_copy(
                    src_ref=x.at[:, src, band, :],
                    dst_ref=x.at[:, dst, band, :],
                    send_sem=halo_send.at[s, 1 + i, h],
                    recv_sem=halo_recv.at[s, 1 + i, h],
                    device_id=neighbours[2 + i][1],
                    device_id_type=MESH,
                ),
            )
            for i, (src, dst) in enumerate(ends)
        ]

    def send_half(s, x, h):
        for there, copy in [row_copy(s, x, h)] + col_copies(s, x, h):

            @pl.when(there)
            def _():
                copy.start()

    pltpu.make_async_copy(
        x1.at[:, inner, pl.ds(TOP, CLAT), :], x1.at[:, inner, pl.ds(TOP, CLAT), :], local.at[9]
    ).wait()
    export(0, x1)

    count = 4
    for there, _ in neighbours:
        count = count + jnp.where(there, 1, 0)
    pl.semaphore_wait(barrier, count)

    for copy in rim_copies(0)[::-1]:
        copy.start()
    for h in range(2):
        send_half(0, x1, h)

    none = jnp.zeros((8, LANES), jnp.float32)

    def clear(g, carry):
        for f in range(FIELDS):
            for s, x in enumerate((x1, x2)):
                x[f, g + 1, TOP - 8 : TOP, :] = none
                x[f, g + 1, TOP + CLAT : TOP + CLAT + 8, :] = none
                hz[s, 0, f, g, 8:16, :] = none
                hz[s, 1, f, g, 0:8, :] = none
        return carry

    lax.fori_loop(0, GROUPS, clear, 0)

    for copy in small[6:]:
        copy.wait()
    total_rows = CLAT * n_lat
    for h in range(2):
        row = (a * CLAT + 8 * h + sub).astype(jnp.float32)
        cosine = jnp.cos((row + 0.5 - 0.5 * total_rows) * (0.5 * math.pi / total_rows))
        metric[h, 0] = 1.0 / (60.0 * cosine)
        metric[h, 1] = 1.0 / (cosine * cosine)

    k_lat = (
        4 * (iota((32, n_lat), 0) & 7)
        + (iota((32, n_lat), 0) >> 3)
        + jnp.where(low_a, 0, n_lat // 2)
    )
    choose_lat = jnp.where(lat_pair[p] == k_lat, 1.0, 0.0).astype(jnp.bfloat16)
    choose_lon = jnp.where(lon_pair[p] == iota((CLAT, n_lon), 0), 1.0, 0.0).astype(jnp.bfloat16)

    def moved_last(placed, row):
        return pltpu.roll(placed[row : row + 8, 4 * LANES :], 64, 1)

    def place_lat(s, side, first_row):
        half = lane < 64
        for f in range(FIELDS):
            got = jnp.concatenate(
                [
                    rl[pl.ds(s * n_lat * BLOCK_ROWS + row, n_lat, stride=BLOCK_ROWS), :]
                    for row in [4 * f + u for u in range(4)] + [4 * FIELDS + f // 2]
                ],
                axis=1,
            )
            placed = None
            for piece in split(got, 3):
                term = dot(choose_lat, piece)
                placed = term if placed is None else placed + term
            for c in range(2):
                plain = [placed[16 * c : 16 * c + 8, u * LANES : (u + 1) * LANES] for u in range(SPAN)]
                moved = [
                    pltpu.roll(placed[16 * c + 8 : 16 * c + 16, u * LANES : (u + 1) * LANES], 64, 1)
                    for u in range(SPAN)
                ]
                if f % 2:
                    plain[4], moved[4] = moved_last(placed, 16 * c), placed[16 * c + 8 : 16 * c + 16, 4 * LANES :]
                tiles = plain[:4] + [jnp.where(half, plain[4], moved[0])]
                tiles += [jnp.where(half, moved[u], moved[u + 1]) for u in range(4)]
                for g, value in enumerate(tiles):
                    hz[s, side, f, 9 * c + g, first_row : first_row + 3, :] = value[0:3]

    def place_lon(s, x, group):
        got = jnp.concatenate(
            [rw[pl.ds(s * n_lon * WIDE_ROWS + f, n_lon, stride=WIDE_ROWS), :] for f in range(FIELDS)], axis=1
        )
        placed = None
        for piece in split(got, 3):
            term = dot(choose_lon, piece)
            placed = term if placed is None else placed + term
        for f in range(FIELDS):
            x[f, group, TOP : TOP + CLAT, :] = placed[:, f * LANES : (f + 1) * LANES]

    def wait_rows(s, h):
        there = jnp.where(h == 0, jnp.logical_not(low_a), jnp.logical_not(high_a))

        @pl.when(there)
        def _():
            row_copy(s, x1, 1 - h)[1].wait_recv()

        @pl.when(jnp.logical_not(there))
        def _():
            got = rl.at[pl.ds(s * n_lat * BLOCK_ROWS, n_lat * BLOCK_ROWS), :]
            pltpu.make_async_copy(got, got, rim_recv.at[s, 0]).wait()

        @pl.when(jnp.logical_and(h == 0, low_a))
        def _():
            place_lat(s, 0, 5)

        @pl.when(jnp.logical_and(h == 1, high_a))
        def _():
            place_lat(s, 1, 8)

    def wait_cols(s, x):
        for h in range(2):
            (west, to_west), (east, to_east) = col_copies(s, x, h)

            @pl.when(west)
            def _():
                to_east.wait_recv()

            @pl.when(east)
            def _():
                to_west.wait_recv()

        @pl.when(lon_edge)
        def _():
            got = rw.at[pl.ds(s * n_lon * WIDE_ROWS, n_lon * WIDE_ROWS), :]
            pltpu.make_async_copy(got, got, rim_recv.at[s, 1]).wait()

        @pl.when(low_b)
        def _():
            place_lon(s, x, 0)

        @pl.when(high_b)
        def _():
            place_lon(s, x, GROUPS + 1)

    not_last = (lane & (LEV - 1)) != LEV - 1
    not_first = (lane & (LEV - 1)) != 0

    def derivatives(x, f, g, r):
        def row(o):
            return x[f, g, pl.ds(r + o, 8), :]

        here = row(0)
        west, east = x[f, g - 1, pl.ds(r, 8), :], x[f, g + 1, pl.ds(r, 8), :]
        up1, down1 = row(1), row(-1)
        lat = (
            0.75 * (up1 - down1) - 0.15 * (row(2) - row(-2)) + (1.0 / 60.0) * (row(3) - row(-3))
        )
        plus1 = pltpu.roll(jnp.where(lane < 32, east, here), 96, 1)
        minus1 = pltpu.roll(jnp.where(lane >= 96, west, here), 32, 1)
        two = pltpu.roll(jnp.where(lane < 64, east - here, here - west), 64, 1)
        plus3 = pltpu.roll(jnp.where(lane < 96, east, here), 32, 1)
        minus3 = pltpu.roll(jnp.where(lane >= 32, west, here), 96, 1)
        lon = 45.0 * (plus1 - minus1) - 9.0 * two + (plus3 - minus3)
        upper = jnp.where(not_last, pltpu.roll(here, LANES - 1, 1), 0.0)
        lower = jnp.where(not_first, pltpu.roll(here, 1, 1), 0.0)
        return here, lat, lon, upper - lower, up1 + down1, plus1 + minus1

    def group_rates(x, g, h, store):
        r = pl.multiple_of(TOP + 8 * h, 8)
        begin = pl.multiple_of((g - 1) * LANES, LANES)
        inv_lon, inv_sq = metric[h, 0], metric[h, 1]
        centre = 2.0 + 2.0 * inv_sq
        u = x[1, g, pl.ds(r, 8), :] * inv_lon
        v = x[2, g, pl.ds(r, 8), :]
        w = x[3, g, pl.ds(r, 8), :] * 0.5
        rho = x[0, g, pl.ds(r, 8), :]
        nu = visc[0, pl.ds(pl.multiple_of(8 * h, 8), 8), pl.ds(begin, LANES)]

        def plain(f):
            here, lat, lon, lev, rows_sum, cols_sum = derivatives(x, f, g, r)
            lap = rows_sum + cols_sum * inv_sq - centre * here
            return here, lat, lon, lev, nu * lap - (u * lon + v * lat + w * lev)

        e, e_lat, e_lon, e_lev, e_rate = plain(4)
        here, _, lon, _, rate = plain(1)
        div = lon * inv_lon
        store(1, g, h, begin, here, rate - KAPPA_PRESS * (e_lon * inv_lon))
        here, lat, _, _, rate = plain(2)
        div = div + lat
        store(2, g, h, begin, here, rate - KAPPA_PRESS * e_lat)
        here, _, _, lev, rate = plain(3)
        div = div + 0.5 * lev
        store(3, g, h, begin, here, rate - (0.5 * KAPPA_PRESS) * e_lev - rho)
        here, _, _, _, rate = plain(0)
        store(0, g, h, begin, here, rate - div)
        store(4, g, h, begin, e, e_rate - GAMMA_HEAT * div)

    def correct(s, x, h, add):
        r = pl.multiple_of(TOP + 8 * h, 8)
        sign = jnp.where(h == 0, -1.0, 1.0)

        def step(k, carry):
            for one in range(2):
                g = 1 + 2 * k + one
                begin = pl.multiple_of((g - 1) * LANES, LANES)
                v = x[2, g, pl.ds(r, 8), :]
                nu = visc[0, pl.ds(pl.multiple_of(8 * h, 8), 8), pl.ds(begin, LANES)]

                def share(f):
                    near, middle, far = (
                        hz[s, h, f, g - 1, pl.ds(jnp.where(h == 0, 8 - o, o), 8), :]
                        for o in (1, 2, 3)
                    )
                    lat = sign * (0.75 * near - 0.15 * middle + (1.0 / 60.0) * far)
                    return lat, nu * near - v * lat

                e_lat, e_rate = share(4)
                v_lat, v_rate = share(2)
                add(2, g, h, begin, v_rate - KAPPA_PRESS * e_lat)
                add(4, g, h, begin, e_rate - GAMMA_HEAT * v_lat)
                add(0, g, h, begin, share(0)[1] - v_lat)
                add(1, g, h, begin, share(1)[1])
                add(3, g, h, begin, share(3)[1])
            return carry

        lax.fori_loop(0, GROUPS // 2, step, 0)

    def section(s, x, store, add):
        def block(i, carry):
            @pl.when(i == 1)
            def _():
                wait_cols(s, x)

            def step(k, inside):
                for one in range(2):
                    g = jnp.where(i == 0, 2 + 2 * (k // 2) + one, 1 + (GROUPS - 1) * one)
                    group_rates(x, g, k % 2, store)
                return inside

            lax.fori_loop(0, jnp.where(i == 0, GROUPS - 2, 2), step, 0)
            return carry

        lax.fori_loop(0, 2, block, 0)

        def side(i, carry):
            h = jnp.where(low_a, 1 - i, i)
            wait_rows(s, h)
            correct(s, x, h, add)
            return carry

        lax.fori_loop(0, 2, side, 0)

    def store_first(f, g, h, begin, here, rate):
        x2[f, g, pl.ds(pl.multiple_of(TOP + 8 * h, 8), 8), :] = here + TIME_STEP * rate

    def store_second(f, g, h, begin, here, rate):
        before = x1[f, g, pl.ds(pl.multiple_of(TOP + 8 * h, 8), 8), :]
        out[0, f, pl.ds(pl.multiple_of(8 * h, 8), 8), pl.ds(begin, LANES)] = 0.5 * (
            before + here + TIME_STEP * rate
        )

    def add_first(f, g, h, begin, rate):
        x2[f, g, pl.ds(pl.multiple_of(TOP + 8 * h, 8), 8), :] += TIME_STEP * rate

    def add_second(f, g, h, begin, rate):
        out[0, f, pl.ds(pl.multiple_of(8 * h, 8), 8), pl.ds(begin, LANES)] += (
            0.5 * TIME_STEP * rate
        )

    section(0, x1, store_first, add_first)
    export(1, x2)
    for copy in rim_copies(1)[::-1]:
        copy.start()
    for h in range(2):
        send_half(1, x2, h)
    section(1, x2, store_second, add_second)

    for s, x in enumerate((x1, x2)):
        for copy in rim_copies(s):
            copy.wait_send()
        for h in range(2):
            for there, copy in [row_copy(s, x, h)] + col_copies(s, x, h):

                @pl.when(there)
                def _():
                    copy.wait_send()


def on_device(*operands):
    n_lat = lax.axis_size("lat")
    n_lon = lax.axis_size("lon")
    operands = list(operands)
    operands[2] = operands[2].reshape(LAT_BLOCK, 1, LANES)
    operands[3] = operands[3].reshape(LON_BLOCK, 1, LANES)
    operands = [pltpu.with_memory_space_constraint(x, pltpu.HBM) for x in operands]

    def body(*refs):
        kernel(n_lat, n_lon, *refs)

    def vmem(*shape):
        return pltpu.VMEM(shape, jnp.float32)

    return pl.pallas_call(
        body,
        out_shape=jax.ShapeDtypeStruct(operands[0].shape, jnp.float32),
        in_specs=[pl.BlockSpec(memory_space=pltpu.HBM)] * 10,
        out_specs=pl.BlockSpec(memory_space=pltpu.VMEM),
        scratch_shapes=[
            vmem(FIELDS, GROUPS + 2, 32, LANES),
            vmem(FIELDS, GROUPS + 2, 32, LANES),
            vmem(2, 2, FIELDS, GROUPS, 16, LANES),
            vmem(1, CLAT, GROUPS * LANES),
            vmem(LAT_BLOCK, 1, LANES),
            vmem(LON_BLOCK, 1, LANES),
            pltpu.SMEM((1, 1, 1, LAT_BLOCK), jnp.float32),
            pltpu.SMEM((1, 1, 1, LON_BLOCK), jnp.float32),
            pltpu.SMEM((1, 1, 1, 2), jnp.int32),
            pltpu.SMEM((1, 1, 1, 2), jnp.int32),
            pltpu.VMEM((2, 1, n_lat), jnp.int32),
            pltpu.VMEM((2, 1, n_lon), jnp.int32),
            vmem(32, 2 * LANES),
            pltpu.VMEM((2, LANES, GROUPS * CLAT), jnp.bfloat16),
            vmem(2, 2, 8, LANES),
            vmem(2, BLOCK_ROWS, LANES),
            vmem(2, 2, WIDE_ROWS, LANES),
            vmem(2 * n_lat * BLOCK_ROWS, LANES),
            vmem(2 * n_lon * WIDE_ROWS, LANES),
            pltpu.SemaphoreType.DMA((10,)),
            pltpu.SemaphoreType.DMA((2, 3, 2)),
            pltpu.SemaphoreType.DMA((2, 3, 2)),
            pltpu.SemaphoreType.DMA((2, 4)),
            pltpu.SemaphoreType.DMA((2, 2)),
        ],
        compiler_params=pltpu.CompilerParams(
            collective_id=0, has_side_effects=True, vmem_limit_bytes=40 * 1024 * 1024
        ),
    )(*operands)


def solution(mesh):
    in_specs = (
        P("yy", None, "lat", "lon"),
        P("yy", "lat", "lon"),
        P("yy", "lat", "lon", None, None),
        P("yy", "lat", "lon", None, None),
        P("yy", "lat", "lon", None),
        P("yy", "lat", "lon", None),
        P("yy", "lat", "lon", None),
        P("yy", "lat", "lon", None),
        P(None, "lon", None),
        P(None, "lat", None),
    )
    out_specs = P("yy", None, "lat", "lon")
    return jax.shard_map(
        on_device, mesh=mesh, in_specs=in_specs, out_specs=out_specs, check_vma=False
    )
```

```python
import math

import jax
import jax.numpy as jnp
from jax import lax
from jax.experimental import pallas as pl
from jax.experimental.pallas import tpu as pltpu
from jax.sharding import PartitionSpec as P

FIELDS = 5
LEV = 32
CLAT = 16
GROUPS = 18
LANES = 128
PATCH_H = 8
PATCH_W = 16
LAT_BLOCK = 18
LON_BLOCK = 6
SPAN = 5
BLOCK_ROWS = 23
WIDE_ROWS = 5
TOP = 8

TIME_STEP = 0.2
KAPPA_PRESS = 0.4
GAMMA_HEAT = 1.4

MESH = pl.DeviceIdType.MESH


def dot(left, right):
    return jnp.dot(left, right, preferred_element_type=jnp.float32)


def iota(shape, axis):
    return lax.broadcasted_iota(jnp.int32, shape, axis)


def split(value, parts):
    pieces = []
    for _ in range(parts):
        piece = value.astype(jnp.bfloat16)
        pieces.append(piece)
        value = value - piece.astype(jnp.float32)
    return pieces


def kernel(
    n_lat,
    n_lon,
    fields_hbm,
    visc_hbm,
    lat_w_hbm,
    lon_w_hbm,
    lat_ang_hbm,
    lon_ang_hbm,
    rows_hbm,
    cols_hbm,
    lat_pair_hbm,
    lon_pair_hbm,
    out,
    x1,
    x2,
    hz,
    visc,
    lat_w,
    lon_w,
    lat_ang,
    lon_ang,
    rows,
    cols,
    lat_pair,
    lon_pair,
    wp,
    mat,
    metric,
    zbuf,
    wbuf,
    rl,
    rw,
    local,
    halo_send,
    halo_recv,
    rim_send,
    rim_recv,
    north_ready,
):
    p = lax.axis_index("yy")
    a = lax.axis_index("lat")
    b = lax.axis_index("lon")
    q = 1 - p
    low_a, high_a = a == 0, a == n_lat - 1
    low_b, high_b = b == 0, b == n_lon - 1
    lon_edge = jnp.logical_or(low_b, high_b)
    neighbours = (
        (jnp.logical_not(low_a), (p, a - 1, b)),
        (jnp.logical_not(high_a), (p, a + 1, b)),
        (jnp.logical_not(low_b), (p, a, b - 1)),
        (jnp.logical_not(high_b), (p, a, b + 1)),
    )

    barrier = pltpu.get_barrier_semaphore()
    for there, device in neighbours:

        @pl.when(there)
        def _():
            pl.semaphore_signal(barrier, inc=1, device_id=device, device_id_type=MESH)

    ring = n_lat // 2

    def signal_sources(semaphore):
        def one(k, carry):
            away = ring // 2 + jnp.where(k % 2 == 1, -((k + 1) // 2), k // 2)
            for part in range(2):
                there = part * ring + lax.rem(a + away, ring)
                pl.semaphore_signal(
                    semaphore, inc=1, device_id=(q, there, b), device_id_type=MESH
                )
            return carry

        lax.fori_loop(0, ring, one, 0)

    @pl.when(low_a)
    def _():
        signal_sources(barrier)

    pl.semaphore_signal(barrier, inc=1, device_id=(q, n_lat - 1, b), device_id_type=MESH)

    @pl.when(lon_edge)
    def _():
        def one(i, carry):
            pl.semaphore_signal(barrier, inc=1, device_id=(q, a, i), device_id_type=MESH)
            return carry

        lax.fori_loop(0, n_lon, one, 0)

    small = [
        pltpu.make_async_copy(src, dst, local.at[i])
        for i, (src, dst) in enumerate(
            (
                (lat_w_hbm, lat_w),
                (lon_w_hbm, lon_w),
                (lat_ang_hbm, lat_ang),
                (lon_ang_hbm, lon_ang),
                (rows_hbm, rows),
                (cols_hbm, cols),
                (lat_pair_hbm, lat_pair),
                (lon_pair_hbm, lon_pair),
                (visc_hbm, visc),
            )
        )
    ]
    for copy in small[:6]:
        copy.start()
    inner = pl.ds(1, GROUPS)
    for g in range(GROUPS):
        pltpu.make_async_copy(
            fields_hbm.at[0, :, :, pl.ds(g * LANES, LANES)],
            x1.at[:, g + 1, pl.ds(TOP, CLAT), :],
            local.at[9],
        ).start()
    for copy in small[6:]:
        copy.start()

    wp[...] = jnp.zeros_like(wp)
    for copy in small[:6]:
        copy.wait()
    for t in range(LAT_BLOCK):
        u, v = t // 4, t % 4
        wp[v * 8 + u : v * 8 + u + 1, 0:LANES] = lat_w[t]
    for t in range(LON_BLOCK):
        u, v = (5, t + 1) if t < 3 else (6, t - 3)
        wp[v * 8 + u : v * 8 + u + 1, LANES : 2 * LANES] = lon_w[t]
    weights = jnp.concatenate(split(wp[...], 3), axis=0)
    entry = iota((2 * LANES, GROUPS * CLAT), 0)
    place = iota((2 * LANES, GROUPS * CLAT), 1)
    is_lon = entry >= LANES
    entry = entry & (LANES - 1)
    row0 = jnp.where(is_lon, rows[0, 0, 0, 1], rows[0, 0, 0, 0])
    col0 = jnp.where(is_lon, cols[0, 0, 0, 1], cols[0, 0, 0, 0])
    from_col = (entry & (PATCH_W - 1)) - 4 * (place >> 4) + col0
    same_row = (place & (CLAT - 1)) - (entry >> 4) == row0
    from_col = jnp.where(same_row, from_col, -1)
    for kk in range(4):
        chosen = jnp.where(from_col == kk, 1.0, 0.0).astype(jnp.bfloat16)
        parts = dot(weights, chosen)
        part = parts[0:32] + parts[32:64] + parts[64:96]
        high, low = split(part, 2)
        mat[0, kk * 32 : (kk + 1) * 32, :] = high
        mat[1, kk * 32 : (kk + 1) * 32, :] = low

    lane = iota((8, LANES), 1)
    sub = iota((8, LANES), 0)
    lane_group = lane >> 5
    target = 4 * sub + lane_group
    angle = jnp.zeros((8, LANES), jnp.float32)
    for t in range(LAT_BLOCK):
        angle = jnp.where(target == t, lat_ang[0, 0, 0, t], angle)
    for t in range(LON_BLOCK):
        u, v = (5, t + 1) if t < 3 else (6, t - 3)
        angle = jnp.where(target == 4 * u + v, lon_ang[0, 0, 0, t], angle)
    cos_angle = jnp.cos(angle)
    sin_angle = jnp.sin(angle)

    def export(s, x):
        columns = []
        for f in range(FIELDS):
            columns.append(x[f, 1 : GROUPS + 1, TOP : TOP + CLAT, :].reshape(GROUPS * CLAT, LANES))
        high, low = split(jnp.concatenate(columns, axis=1), 2)
        total = dot(mat[0], high) + dot(mat[0], low) + dot(mat[1], high)
        blocks = []
        for f in range(FIELDS):
            piece = total[:, f * LANES : (f + 1) * LANES]
            result = None
            for shift in range(4):
                mixed = None
                for kk in range(4):
                    v = (kk + shift) % 4
                    part = piece[kk * 32 + v * 8 : kk * 32 + v * 8 + 8, :]
                    mixed = part if mixed is None else jnp.where(lane_group == kk, part, mixed)
                if shift:
                    mixed = pltpu.roll(mixed, 32 * shift, 1)
                result = mixed if result is None else result + mixed
            blocks.append(result)
        east = cos_angle * blocks[1] + sin_angle * blocks[2]
        north = cos_angle * blocks[2] - sin_angle * blocks[1]
        blocks[1], blocks[2] = east, north
        for f in range(FIELDS):
            zbuf[s, 4 * f : 4 * f + 4, :] = blocks[f][0:4]
            last = blocks[f][4:5]
            if f % 2 == 0 and f + 1 < FIELDS:
                last = jnp.where(
                    lane[0:1] < 64, last, pltpu.roll(blocks[f + 1], 64, 1)[4:5]
                )
            if f % 2 == 0:
                zbuf[s, 4 * FIELDS + f // 2 : 4 * FIELDS + f // 2 + 1, :] = last
            wbuf[s, 0, f : f + 1, :] = blocks[f][5:6]
            wbuf[s, 1, f : f + 1, :] = blocks[f][6:7]

    def rim_copies(s, which=(3, 2, 1, 0)):
        lat_dst = rl.at[pl.ds((s * n_lat + a) * BLOCK_ROWS, BLOCK_ROWS), :]
        lon_dst = rw.at[pl.ds((s * n_lon + b) * WIDE_ROWS, WIDE_ROWS), :]
        ends = (
            (zbuf.at[s], lat_dst, (q, 0, b), 0),
            (zbuf.at[s], lat_dst, (q, n_lat - 1, b), 0),
            (wbuf.at[s, 0], lon_dst, (q, a, 0), 1),
            (wbuf.at[s, 1], lon_dst, (q, a, n_lon - 1), 1),
        )
        return [
            pltpu.make_async_remote_copy(
                src_ref=src,
                dst_ref=dst,
                send_sem=rim_send.at[s, i],
                recv_sem=rim_recv.at[s, kind],
                device_id=device,
                device_id_type=MESH,
            )
            for i, (src, dst, device, kind) in [(i, ends[i]) for i in which]
        ]

    def row_copy(s, x, h):
        there = jnp.where(h == 0, jnp.logical_not(low_a), jnp.logical_not(high_a))
        return there, pltpu.make_async_remote_copy(
            src_ref=x.at[:, inner, pl.ds(TOP + (CLAT - 3) * h, 3), :],
            dst_ref=hz.at[s, 1 - h, :, :, pl.ds(8 - 3 * h, 3), :],
            send_sem=halo_send.at[s, 0, h],
            recv_sem=halo_recv.at[s, 0, h],
            device_id=(p, a + 2 * h - 1, b),
            device_id_type=MESH,
        )

    def col_copies(s, x, h):
        band = pl.ds(pl.multiple_of(TOP + 8 * h, 8), 8)
        ends = ((1, GROUPS + 1), (GROUPS, 0))
        return [
            (
                neighbours[2 + i][0],
                pltpu.make_async_remote_copy(
                    src_ref=x.at[:, src, band, :],
                    dst_ref=x.at[:, dst, band, :],
                    send_sem=halo_send.at[s, 1 + i, h],
                    recv_sem=halo_recv.at[s, 1 + i, h],
                    device_id=neighbours[2 + i][1],
                    device_id_type=MESH,
                ),
            )
            for i, (src, dst) in enumerate(ends)
        ]

    def send_half(s, x, h):
        for there, copy in [row_copy(s, x, h)] + col_copies(s, x, h):

            @pl.when(there)
            def _():
                copy.start()

    pltpu.make_async_copy(
        x1.at[:, inner, pl.ds(TOP, CLAT), :], x1.at[:, inner, pl.ds(TOP, CLAT), :], local.at[9]
    ).wait()
    export(0, x1)

    count = 3 + jnp.where(high_a, n_lat, 0)
    for there, _ in neighbours:
        count = count + jnp.where(there, 1, 0)
    pl.semaphore_wait(barrier, count)

    @pl.when(high_a)
    def _():
        signal_sources(north_ready)

    for copy in rim_copies(0, (3, 2, 0)):
        copy.start()
    for h in range(2):
        send_half(0, x1, h)

    none = jnp.zeros((8, LANES), jnp.float32)

    def clear(g, carry):
        for f in range(FIELDS):
            for s, x in enumerate((x1, x2)):
                x[f, g + 1, TOP - 8 : TOP, :] = none
                x[f, g + 1, TOP + CLAT : TOP + CLAT + 8, :] = none
                hz[s, 0, f, g, 8:16, :] = none
                hz[s, 1, f, g, 0:8, :] = none
        return carry

    lax.fori_loop(0, GROUPS, clear, 0)

    for copy in small[6:]:
        copy.wait()
    total_rows = CLAT * n_lat
    for h in range(2):
        row = (a * CLAT + 8 * h + sub).astype(jnp.float32)
        cosine = jnp.cos((row + 0.5 - 0.5 * total_rows) * (0.5 * math.pi / total_rows))
        metric[h, 0] = 1.0 / (60.0 * cosine)
        metric[h, 1] = 1.0 / (cosine * cosine)

    k_lat = (
        4 * (iota((32, n_lat), 0) & 7)
        + (iota((32, n_lat), 0) >> 3)
        + jnp.where(low_a, 0, n_lat // 2)
    )
    choose_lat = jnp.where(lat_pair[p] == k_lat, 1.0, 0.0).astype(jnp.bfloat16)
    choose_lon = jnp.where(lon_pair[p] == iota((CLAT, n_lon), 0), 1.0, 0.0).astype(jnp.bfloat16)

    def moved_last(placed, row):
        return pltpu.roll(placed[row : row + 8, 4 * LANES :], 64, 1)

    def place_lat(s, side, first_row):
        half = lane < 64
        for f in range(FIELDS):
            got = jnp.concatenate(
                [
                    rl[pl.ds(s * n_lat * BLOCK_ROWS + row, n_lat, stride=BLOCK_ROWS), :]
                    for row in [4 * f + u for u in range(4)] + [4 * FIELDS + f // 2]
                ],
                axis=1,
            )
            placed = None
            for piece in split(got, 3):
                term = dot(choose_lat, piece)
                placed = term if placed is None else placed + term
            for c in range(2):
                plain = [placed[16 * c : 16 * c + 8, u * LANES : (u + 1) * LANES] for u in range(SPAN)]
                moved = [
                    pltpu.roll(placed[16 * c + 8 : 16 * c + 16, u * LANES : (u + 1) * LANES], 64, 1)
                    for u in range(SPAN)
                ]
                if f % 2:
                    plain[4], moved[4] = moved_last(placed, 16 * c), placed[16 * c + 8 : 16 * c + 16, 4 * LANES :]
                tiles = plain[:4] + [jnp.where(half, plain[4], moved[0])]
                tiles += [jnp.where(half, moved[u], moved[u + 1]) for u in range(4)]
                for g, value in enumerate(tiles):
                    hz[s, side, f, 9 * c + g, first_row : first_row + 3, :] = value[0:3]

    def place_lon(s, x, group):
        got = jnp.concatenate(
            [rw[pl.ds(s * n_lon * WIDE_ROWS + f, n_lon, stride=WIDE_ROWS), :] for f in range(FIELDS)], axis=1
        )
        placed = None
        for piece in split(got, 3):
            term = dot(choose_lon, piece)
            placed = term if placed is None else placed + term
        for f in range(FIELDS):
            x[f, group, TOP : TOP + CLAT, :] = placed[:, f * LANES : (f + 1) * LANES]

    def wait_rows(s, h):
        there = jnp.where(h == 0, jnp.logical_not(low_a), jnp.logical_not(high_a))

        @pl.when(there)
        def _():
            row_copy(s, x1, 1 - h)[1].wait_recv()

        @pl.when(jnp.logical_not(there))
        def _():
            got = rl.at[pl.ds(s * n_lat * BLOCK_ROWS, n_lat * BLOCK_ROWS), :]
            pltpu.make_async_copy(got, got, rim_recv.at[s, 0]).wait()

        @pl.when(jnp.logical_and(h == 0, low_a))
        def _():
            place_lat(s, 0, 5)

        @pl.when(jnp.logical_and(h == 1, high_a))
        def _():
            place_lat(s, 1, 8)

    def wait_cols(s, x):
        for h in range(2):
            (west, to_west), (east, to_east) = col_copies(s, x, h)

            @pl.when(west)
            def _():
                to_east.wait_recv()

            @pl.when(east)
            def _():
                to_west.wait_recv()

        @pl.when(lon_edge)
        def _():
            got = rw.at[pl.ds(s * n_lon * WIDE_ROWS, n_lon * WIDE_ROWS), :]
            pltpu.make_async_copy(got, got, rim_recv.at[s, 1]).wait()

        @pl.when(low_b)
        def _():
            place_lon(s, x, 0)

        @pl.when(high_b)
        def _():
            place_lon(s, x, GROUPS + 1)

    not_last = (lane & (LEV - 1)) != LEV - 1
    not_first = (lane & (LEV - 1)) != 0

    def derivatives(x, f, g, r):
        def row(o):
            return x[f, g, pl.ds(r + o, 8), :]

        here = row(0)
        west, east = x[f, g - 1, pl.ds(r, 8), :], x[f, g + 1, pl.ds(r, 8), :]
        up1, down1 = row(1), row(-1)
        lat = (
            0.75 * (up1 - down1) - 0.15 * (row(2) - row(-2)) + (1.0 / 60.0) * (row(3) - row(-3))
        )
        plus1 = pltpu.roll(jnp.where(lane < 32, east, here), 96, 1)
        minus1 = pltpu.roll(jnp.where(lane >= 96, west, here), 32, 1)
        two = pltpu.roll(jnp.where(lane < 64, east - here, here - west), 64, 1)
        plus3 = pltpu.roll(jnp.where(lane < 96, east, here), 32, 1)
        minus3 = pltpu.roll(jnp.where(lane >= 32, west, here), 96, 1)
        lon = 45.0 * (plus1 - minus1) - 9.0 * two + (plus3 - minus3)
        upper = jnp.where(not_last, pltpu.roll(here, LANES - 1, 1), 0.0)
        lower = jnp.where(not_first, pltpu.roll(here, 1, 1), 0.0)
        return here, lat, lon, upper - lower, up1 + down1, plus1 + minus1

    def group_rates(x, g, h, store):
        r = pl.multiple_of(TOP + 8 * h, 8)
        begin = pl.multiple_of((g - 1) * LANES, LANES)
        inv_lon, inv_sq = metric[h, 0], metric[h, 1]
        centre = 2.0 + 2.0 * inv_sq
        u = x[1, g, pl.ds(r, 8), :] * inv_lon
        v = x[2, g, pl.ds(r, 8), :]
        w = x[3, g, pl.ds(r, 8), :] * 0.5
        rho = x[0, g, pl.ds(r, 8), :]
        nu = visc[0, pl.ds(pl.multiple_of(8 * h, 8), 8), pl.ds(begin, LANES)]

        def plain(f):
            here, lat, lon, lev, rows_sum, cols_sum = derivatives(x, f, g, r)
            lap = rows_sum + cols_sum * inv_sq - centre * here
            return here, lat, lon, lev, nu * lap - (u * lon + v * lat + w * lev)

        e, e_lat, e_lon, e_lev, e_rate = plain(4)
        here, _, lon, _, rate = plain(1)
        div = lon * inv_lon
        store(1, g, h, begin, here, rate - KAPPA_PRESS * (e_lon * inv_lon))
        here, lat, _, _, rate = plain(2)
        div = div + lat
        store(2, g, h, begin, here, rate - KAPPA_PRESS * e_lat)
        here, _, _, lev, rate = plain(3)
        div = div + 0.5 * lev
        store(3, g, h, begin, here, rate - (0.5 * KAPPA_PRESS) * e_lev - rho)
        here, _, _, _, rate = plain(0)
        store(0, g, h, begin, here, rate - div)
        store(4, g, h, begin, e, e_rate - GAMMA_HEAT * div)

    def correct(s, x, h, add):
        r = pl.multiple_of(TOP + 8 * h, 8)
        sign = jnp.where(h == 0, -1.0, 1.0)

        def step(k, carry):
            for one in range(2):
                g = 1 + 2 * k + one
                begin = pl.multiple_of((g - 1) * LANES, LANES)
                v = x[2, g, pl.ds(r, 8), :]
                nu = visc[0, pl.ds(pl.multiple_of(8 * h, 8), 8), pl.ds(begin, LANES)]

                def share(f):
                    near, middle, far = (
                        hz[s, h, f, g - 1, pl.ds(jnp.where(h == 0, 8 - o, o), 8), :]
                        for o in (1, 2, 3)
                    )
                    lat = sign * (0.75 * near - 0.15 * middle + (1.0 / 60.0) * far)
                    return lat, nu * near - v * lat

                e_lat, e_rate = share(4)
                v_lat, v_rate = share(2)
                add(2, g, h, begin, v_rate - KAPPA_PRESS * e_lat)
                add(4, g, h, begin, e_rate - GAMMA_HEAT * v_lat)
                add(0, g, h, begin, share(0)[1] - v_lat)
                add(1, g, h, begin, share(1)[1])
                add(3, g, h, begin, share(3)[1])
            return carry

        lax.fori_loop(0, GROUPS // 2, step, 0)

    def section(s, x, store, add):
        def block(i, carry):
            @pl.when(i == 1)
            def _():
                if s == 0:
                    pl.semaphore_wait(north_ready, 1)
                    rim_copies(0, (1,))[0].start()
                wait_cols(s, x)

            def step(k, inside):
                for one in range(2):
                    g = jnp.where(i == 0, 2 + 2 * (k // 2) + one, 1 + (GROUPS - 1) * one)
                    group_rates(x, g, k % 2, store)
                return inside

            lax.fori_loop(0, jnp.where(i == 0, GROUPS - 2, 2), step, 0)
            return carry

        lax.fori_loop(0, 2, block, 0)

        def side(i, carry):
            h = jnp.where(low_a, 1 - i, i)
            wait_rows(s, h)
            correct(s, x, h, add)
            return carry

        lax.fori_loop(0, 2, side, 0)

    def store_first(f, g, h, begin, here, rate):
        x2[f, g, pl.ds(pl.multiple_of(TOP + 8 * h, 8), 8), :] = here + TIME_STEP * rate

    def store_second(f, g, h, begin, here, rate):
        before = x1[f, g, pl.ds(pl.multiple_of(TOP + 8 * h, 8), 8), :]
        out[0, f, pl.ds(pl.multiple_of(8 * h, 8), 8), pl.ds(begin, LANES)] = 0.5 * (
            before + here + TIME_STEP * rate
        )

    def add_first(f, g, h, begin, rate):
        x2[f, g, pl.ds(pl.multiple_of(TOP + 8 * h, 8), 8), :] += TIME_STEP * rate

    def add_second(f, g, h, begin, rate):
        out[0, f, pl.ds(pl.multiple_of(8 * h, 8), 8), pl.ds(begin, LANES)] += (
            0.5 * TIME_STEP * rate
        )

    section(0, x1, store_first, add_first)
    export(1, x2)
    for copy in rim_copies(1):
        copy.start()
    for h in range(2):
        send_half(1, x2, h)
    section(1, x2, store_second, add_second)

    for s, x in enumerate((x1, x2)):
        for copy in rim_copies(s):
            copy.wait_send()
        for h in range(2):
            for there, copy in [row_copy(s, x, h)] + col_copies(s, x, h):

                @pl.when(there)
                def _():
                    copy.wait_send()


def on_device(*operands):
    n_lat = lax.axis_size("lat")
    n_lon = lax.axis_size("lon")
    operands = list(operands)
    operands[2] = operands[2].reshape(LAT_BLOCK, 1, LANES)
    operands[3] = operands[3].reshape(LON_BLOCK, 1, LANES)
    operands = [pltpu.with_memory_space_constraint(x, pltpu.HBM) for x in operands]

    def body(*refs):
        kernel(n_lat, n_lon, *refs)

    def vmem(*shape):
        return pltpu.VMEM(shape, jnp.float32)

    return pl.pallas_call(
        body,
        out_shape=jax.ShapeDtypeStruct(operands[0].shape, jnp.float32),
        in_specs=[pl.BlockSpec(memory_space=pltpu.HBM)] * 10,
        out_specs=pl.BlockSpec(memory_space=pltpu.VMEM),
        scratch_shapes=[
            vmem(FIELDS, GROUPS + 2, 32, LANES),
            vmem(FIELDS, GROUPS + 2, 32, LANES),
            vmem(2, 2, FIELDS, GROUPS, 16, LANES),
            vmem(1, CLAT, GROUPS * LANES),
            vmem(LAT_BLOCK, 1, LANES),
            vmem(LON_BLOCK, 1, LANES),
            pltpu.SMEM((1, 1, 1, LAT_BLOCK), jnp.float32),
            pltpu.SMEM((1, 1, 1, LON_BLOCK), jnp.float32),
            pltpu.SMEM((1, 1, 1, 2), jnp.int32),
            pltpu.SMEM((1, 1, 1, 2), jnp.int32),
            pltpu.VMEM((2, 1, n_lat), jnp.int32),
            pltpu.VMEM((2, 1, n_lon), jnp.int32),
            vmem(32, 2 * LANES),
            pltpu.VMEM((2, LANES, GROUPS * CLAT), jnp.bfloat16),
            vmem(2, 2, 8, LANES),
            vmem(2, BLOCK_ROWS, LANES),
            vmem(2, 2, WIDE_ROWS, LANES),
            vmem(2 * n_lat * BLOCK_ROWS, LANES),
            vmem(2 * n_lon * WIDE_ROWS, LANES),
            pltpu.SemaphoreType.DMA((10,)),
            pltpu.SemaphoreType.DMA((2, 3, 2)),
            pltpu.SemaphoreType.DMA((2, 3, 2)),
            pltpu.SemaphoreType.DMA((2, 4)),
            pltpu.SemaphoreType.DMA((2, 2)),
            pltpu.SemaphoreType.REGULAR,
        ],
        compiler_params=pltpu.CompilerParams(
            collective_id=0, has_side_effects=True, vmem_limit_bytes=40 * 1024 * 1024
        ),
    )(*operands)


def solution(mesh):
    in_specs = (
        P("yy", None, "lat", "lon"),
        P("yy", "lat", "lon"),
        P("yy", "lat", "lon", None, None),
        P("yy", "lat", "lon", None, None),
        P("yy", "lat", "lon", None),
        P("yy", "lat", "lon", None),
        P("yy", "lat", "lon", None),
        P("yy", "lat", "lon", None),
        P(None, "lon", None),
        P(None, "lat", None),
    )
    out_specs = P("yy", None, "lat", "lon")
    return jax.shard_map(
        on_device, mesh=mesh, in_specs=in_specs, out_specs=out_specs, check_vma=False
    )
```

```python
import math

import jax
import jax.numpy as jnp
from jax import lax
from jax.experimental import pallas as pl
from jax.experimental.pallas import tpu as pltpu
from jax.sharding import PartitionSpec as P

FIELDS = 5
LEV = 32
CLAT = 16
GROUPS = 18
LANES = 128
PATCH_H = 8
PATCH_W = 16
LAT_BLOCK = 18
LON_BLOCK = 6
SPAN = 5
BLOCK_ROWS = 23
WIDE_ROWS = 5
TOP = 8

TIME_STEP = 0.2
KAPPA_PRESS = 0.4
GAMMA_HEAT = 1.4

MESH = pl.DeviceIdType.MESH


def dot(left, right):
    return jnp.dot(left, right, preferred_element_type=jnp.float32)


def iota(shape, axis):
    return lax.broadcasted_iota(jnp.int32, shape, axis)


def split(value, parts):
    pieces = []
    for _ in range(parts):
        piece = value.astype(jnp.bfloat16)
        pieces.append(piece)
        value = value - piece.astype(jnp.float32)
    return pieces


def kernel(
    n_lat,
    n_lon,
    fields_hbm,
    visc_hbm,
    lat_w_hbm,
    lon_w_hbm,
    lat_ang_hbm,
    lon_ang_hbm,
    rows_hbm,
    cols_hbm,
    lat_pair_hbm,
    lon_pair_hbm,
    out,
    x1,
    x2,
    hz,
    visc,
    lat_w,
    lon_w,
    lat_ang,
    lon_ang,
    rows,
    cols,
    lat_pair,
    lon_pair,
    wp,
    mat,
    metric,
    zbuf,
    wbuf,
    rl,
    rw,
    local,
    halo_send,
    halo_recv,
    rim_send,
    rim_recv,
    north_ready,
):
    p = lax.axis_index("yy")
    a = lax.axis_index("lat")
    b = lax.axis_index("lon")
    q = 1 - p
    low_a, high_a = a == 0, a == n_lat - 1
    low_b, high_b = b == 0, b == n_lon - 1
    lon_edge = jnp.logical_or(low_b, high_b)
    neighbours = (
        (jnp.logical_not(low_a), (p, a - 1, b)),
        (jnp.logical_not(high_a), (p, a + 1, b)),
        (jnp.logical_not(low_b), (p, a, b - 1)),
        (jnp.logical_not(high_b), (p, a, b + 1)),
    )

    barrier = pltpu.get_barrier_semaphore()
    for there, device in neighbours:

        @pl.when(there)
        def _():
            pl.semaphore_signal(barrier, inc=1, device_id=device, device_id_type=MESH)

    ring = n_lat // 2

    def signal_sources(semaphore):
        def one(k, carry):
            away = ring // 2 + jnp.where(k % 2 == 1, -((k + 1) // 2), k // 2)
            for part in range(2):
                there = part * ring + lax.rem(a + away, ring)
                pl.semaphore_signal(
                    semaphore, inc=1, device_id=(q, there, b), device_id_type=MESH
                )
            return carry

        lax.fori_loop(0, ring, one, 0)

    @pl.when(low_a)
    def _():
        signal_sources(barrier)

    pl.semaphore_signal(barrier, inc=1, device_id=(q, n_lat - 1, b), device_id_type=MESH)

    @pl.when(lon_edge)
    def _():
        def one(i, carry):
            pl.semaphore_signal(barrier, inc=1, device_id=(q, a, i), device_id_type=MESH)
            return carry

        lax.fori_loop(0, n_lon, one, 0)

    small = [
        pltpu.make_async_copy(src, dst, local.at[i])
        for i, (src, dst) in enumerate(
            (
                (lat_w_hbm, lat_w),
                (lon_w_hbm, lon_w),
                (lat_ang_hbm, lat_ang),
                (lon_ang_hbm, lon_ang),
                (rows_hbm, rows),
                (cols_hbm, cols),
                (lat_pair_hbm, lat_pair),
                (lon_pair_hbm, lon_pair),
                (visc_hbm, visc),
            )
        )
    ]
    for copy in small[:6]:
        copy.start()
    inner = pl.ds(1, GROUPS)
    for g in range(GROUPS):
        pltpu.make_async_copy(
            fields_hbm.at[0, :, :, pl.ds(g * LANES, LANES)],
            x1.at[:, g + 1, pl.ds(TOP, CLAT), :],
            local.at[9],
        ).start()
    for copy in small[6:]:
        copy.start()

    count = 3 + jnp.where(high_a, n_lat, 0)
    for there, _ in neighbours:
        count = count + jnp.where(there, 1, 0)

    @pl.when(high_a)
    def _():
        pl.semaphore_wait(barrier, count)
        signal_sources(north_ready)

    wp[...] = jnp.zeros_like(wp)
    for copy in small[:6]:
        copy.wait()
    for t in range(LAT_BLOCK):
        u, v = t // 4, t % 4
        wp[v * 8 + u : v * 8 + u + 1, 0:LANES] = lat_w[t]
    for t in range(LON_BLOCK):
        u, v = (5, t + 1) if t < 3 else (6, t - 3)
        wp[v * 8 + u : v * 8 + u + 1, LANES : 2 * LANES] = lon_w[t]
    weights = jnp.concatenate(split(wp[...], 3), axis=0)
    entry = iota((2 * LANES, GROUPS * CLAT), 0)
    place = iota((2 * LANES, GROUPS * CLAT), 1)
    is_lon = entry >= LANES
    entry = entry & (LANES - 1)
    row0 = jnp.where(is_lon, rows[0, 0, 0, 1], rows[0, 0, 0, 0])
    col0 = jnp.where(is_lon, cols[0, 0, 0, 1], cols[0, 0, 0, 0])
    from_col = (entry & (PATCH_W - 1)) - 4 * (place >> 4) + col0
    same_row = (place & (CLAT - 1)) - (entry >> 4) == row0
    from_col = jnp.where(same_row, from_col, -1)
    for kk in range(4):
        chosen = jnp.where(from_col == kk, 1.0, 0.0).astype(jnp.bfloat16)
        parts = dot(weights, chosen)
        part = parts[0:32] + parts[32:64] + parts[64:96]
        high, low = split(part, 2)
        mat[0, kk * 32 : (kk + 1) * 32, :] = high
        mat[1, kk * 32 : (kk + 1) * 32, :] = low

    lane = iota((8, LANES), 1)
    sub = iota((8, LANES), 0)
    lane_group = lane >> 5
    target = 4 * sub + lane_group
    angle = jnp.zeros((8, LANES), jnp.float32)
    for t in range(LAT_BLOCK):
        angle = jnp.where(target == t, lat_ang[0, 0, 0, t], angle)
    for t in range(LON_BLOCK):
        u, v = (5, t + 1) if t < 3 else (6, t - 3)
        angle = jnp.where(target == 4 * u + v, lon_ang[0, 0, 0, t], angle)
    cos_angle = jnp.cos(angle)
    sin_angle = jnp.sin(angle)

    def export(s, x):
        columns = []
        for f in range(FIELDS):
            columns.append(x[f, 1 : GROUPS + 1, TOP : TOP + CLAT, :].reshape(GROUPS * CLAT, LANES))
        high, low = split(jnp.concatenate(columns, axis=1), 2)
        total = dot(mat[0], high) + dot(mat[0], low) + dot(mat[1], high)
        blocks = []
        for f in range(FIELDS):
            piece = total[:, f * LANES : (f + 1) * LANES]
            result = None
            for shift in range(4):
                mixed = None
                for kk in range(4):
                    v = (kk + shift) % 4
                    part = piece[kk * 32 + v * 8 : kk * 32 + v * 8 + 8, :]
                    mixed = part if mixed is None else jnp.where(lane_group == kk, part, mixed)
                if shift:
                    mixed = pltpu.roll(mixed, 32 * shift, 1)
                result = mixed if result is None else result + mixed
            blocks.append(result)
        east = cos_angle * blocks[1] + sin_angle * blocks[2]
        north = cos_angle * blocks[2] - sin_angle * blocks[1]
        blocks[1], blocks[2] = east, north
        for f in range(FIELDS):
            zbuf[s, 4 * f : 4 * f + 4, :] = blocks[f][0:4]
            last = blocks[f][4:5]
            if f % 2 == 0 and f + 1 < FIELDS:
                last = jnp.where(
                    lane[0:1] < 64, last, pltpu.roll(blocks[f + 1], 64, 1)[4:5]
                )
            if f % 2 == 0:
                zbuf[s, 4 * FIELDS + f // 2 : 4 * FIELDS + f // 2 + 1, :] = last
            wbuf[s, 0, f : f + 1, :] = blocks[f][5:6]
            wbuf[s, 1, f : f + 1, :] = blocks[f][6:7]

    def rim_copies(s, which=(3, 2, 1, 0)):
        lat_dst = rl.at[pl.ds((s * n_lat + a) * BLOCK_ROWS, BLOCK_ROWS), :]
        lon_dst = rw.at[pl.ds((s * n_lon + b) * WIDE_ROWS, WIDE_ROWS), :]
        ends = (
            (zbuf.at[s], lat_dst, (q, 0, b), 0),
            (zbuf.at[s], lat_dst, (q, n_lat - 1, b), 0),
            (wbuf.at[s, 0], lon_dst, (q, a, 0), 1),
            (wbuf.at[s, 1], lon_dst, (q, a, n_lon - 1), 1),
        )
        return [
            pltpu.make_async_remote_copy(
                src_ref=src,
                dst_ref=dst,
                send_sem=rim_send.at[s, i],
                recv_sem=rim_recv.at[s, kind],
                device_id=device,
                device_id_type=MESH,
            )
            for i, (src, dst, device, kind) in [(i, ends[i]) for i in which]
        ]

    def row_copy(s, x, h):
        there = jnp.where(h == 0, jnp.logical_not(low_a), jnp.logical_not(high_a))
        return there, pltpu.make_async_remote_copy(
            src_ref=x.at[:, inner, pl.ds(TOP + (CLAT - 3) * h, 3), :],
            dst_ref=hz.at[s, 1 - h, :, :, pl.ds(8 - 3 * h, 3), :],
            send_sem=halo_send.at[s, 0, h],
            recv_sem=halo_recv.at[s, 0, h],
            device_id=(p, a + 2 * h - 1, b),
            device_id_type=MESH,
        )

    def col_copies(s, x, h):
        band = pl.ds(pl.multiple_of(TOP + 8 * h, 8), 8)
        ends = ((1, GROUPS + 1), (GROUPS, 0))
        return [
            (
                neighbours[2 + i][0],
                pltpu.make_async_remote_copy(
                    src_ref=x.at[:, src, band, :],
                    dst_ref=x.at[:, dst, band, :],
                    send_sem=halo_send.at[s, 1 + i, h],
                    recv_sem=halo_recv.at[s, 1 + i, h],
                    device_id=neighbours[2 + i][1],
                    device_id_type=MESH,
                ),
            )
            for i, (src, dst) in enumerate(ends)
        ]

    def send_half(s, x, h):
        for there, copy in [row_copy(s, x, h)] + col_copies(s, x, h):

            @pl.when(there)
            def _():
                copy.start()

    pltpu.make_async_copy(
        x1.at[:, inner, pl.ds(TOP, CLAT), :], x1.at[:, inner, pl.ds(TOP, CLAT), :], local.at[9]
    ).wait()
    export(0, x1)

    @pl.when(jnp.logical_not(high_a))
    def _():
        pl.semaphore_wait(barrier, count)

    for copy in rim_copies(0, (3, 2, 0)):
        copy.start()
    for h in range(2):
        send_half(0, x1, h)

    none = jnp.zeros((8, LANES), jnp.float32)

    def clear(g, carry):
        for f in range(FIELDS):
            for s, x in enumerate((x1, x2)):
                x[f, g + 1, TOP - 8 : TOP, :] = none
                x[f, g + 1, TOP + CLAT : TOP + CLAT + 8, :] = none
                hz[s, 0, f, g, 8:16, :] = none
                hz[s, 1, f, g, 0:8, :] = none
        return carry

    lax.fori_loop(0, GROUPS, clear, 0)

    for copy in small[6:]:
        copy.wait()
    total_rows = CLAT * n_lat
    for h in range(2):
        row = (a * CLAT + 8 * h + sub).astype(jnp.float32)
        cosine = jnp.cos((row + 0.5 - 0.5 * total_rows) * (0.5 * math.pi / total_rows))
        metric[h, 0] = 1.0 / (60.0 * cosine)
        metric[h, 1] = 1.0 / (cosine * cosine)

    k_lat = (
        4 * (iota((32, n_lat), 0) & 7)
        + (iota((32, n_lat), 0) >> 3)
        + jnp.where(low_a, 0, n_lat // 2)
    )
    choose_lat = jnp.where(lat_pair[p] == k_lat, 1.0, 0.0).astype(jnp.bfloat16)
    choose_lon = jnp.where(lon_pair[p] == iota((CLAT, n_lon), 0), 1.0, 0.0).astype(jnp.bfloat16)

    def moved_last(placed, row):
        return pltpu.roll(placed[row : row + 8, 4 * LANES :], 64, 1)

    def place_lat(s, side, first_row):
        half = lane < 64
        for f in range(FIELDS):
            got = jnp.concatenate(
                [
                    rl[pl.ds(s * n_lat * BLOCK_ROWS + row, n_lat, stride=BLOCK_ROWS), :]
                    for row in [4 * f + u for u in range(4)] + [4 * FIELDS + f // 2]
                ],
                axis=1,
            )
            placed = None
            for piece in split(got, 3):
                term = dot(choose_lat, piece)
                placed = term if placed is None else placed + term
            for c in range(2):
                plain = [placed[16 * c : 16 * c + 8, u * LANES : (u + 1) * LANES] for u in range(SPAN)]
                moved = [
                    pltpu.roll(placed[16 * c + 8 : 16 * c + 16, u * LANES : (u + 1) * LANES], 64, 1)
                    for u in range(SPAN)
                ]
                if f % 2:
                    plain[4], moved[4] = moved_last(placed, 16 * c), placed[16 * c + 8 : 16 * c + 16, 4 * LANES :]
                tiles = plain[:4] + [jnp.where(half, plain[4], moved[0])]
                tiles += [jnp.where(half, moved[u], moved[u + 1]) for u in range(4)]
                for g, value in enumerate(tiles):
                    hz[s, side, f, 9 * c + g, first_row : first_row + 3, :] = value[0:3]

    def place_lon(s, x, group):
        got = jnp.concatenate(
            [rw[pl.ds(s * n_lon * WIDE_ROWS + f, n_lon, stride=WIDE_ROWS), :] for f in range(FIELDS)], axis=1
        )
        placed = None
        for piece in split(got, 3):
            term = dot(choose_lon, piece)
            placed = term if placed is None else placed + term
        for f in range(FIELDS):
            x[f, group, TOP : TOP + CLAT, :] = placed[:, f * LANES : (f + 1) * LANES]

    def wait_rows(s, h):
        there = jnp.where(h == 0, jnp.logical_not(low_a), jnp.logical_not(high_a))

        @pl.when(there)
        def _():
            row_copy(s, x1, 1 - h)[1].wait_recv()

        @pl.when(jnp.logical_not(there))
        def _():
            got = rl.at[pl.ds(s * n_lat * BLOCK_ROWS, n_lat * BLOCK_ROWS), :]
            pltpu.make_async_copy(got, got, rim_recv.at[s, 0]).wait()

        @pl.when(jnp.logical_and(h == 0, low_a))
        def _():
            place_lat(s, 0, 5)

        @pl.when(jnp.logical_and(h == 1, high_a))
        def _():
            place_lat(s, 1, 8)

    def wait_cols(s, x):
        for h in range(2):
            (west, to_west), (east, to_east) = col_copies(s, x, h)

            @pl.when(west)
            def _():
                to_east.wait_recv()

            @pl.when(east)
            def _():
                to_west.wait_recv()

        @pl.when(lon_edge)
        def _():
            got = rw.at[pl.ds(s * n_lon * WIDE_ROWS, n_lon * WIDE_ROWS), :]
            pltpu.make_async_copy(got, got, rim_recv.at[s, 1]).wait()

        @pl.when(low_b)
        def _():
            place_lon(s, x, 0)

        @pl.when(high_b)
        def _():
            place_lon(s, x, GROUPS + 1)

    not_last = (lane & (LEV - 1)) != LEV - 1
    not_first = (lane & (LEV - 1)) != 0

    def derivatives(x, f, g, r):
        def row(o):
            return x[f, g, pl.ds(r + o, 8), :]

        here = row(0)
        west, east = x[f, g - 1, pl.ds(r, 8), :], x[f, g + 1, pl.ds(r, 8), :]
        up1, down1 = row(1), row(-1)
        lat = (
            0.75 * (up1 - down1) - 0.15 * (row(2) - row(-2)) + (1.0 / 60.0) * (row(3) - row(-3))
        )
        plus1 = pltpu.roll(jnp.where(lane < 32, east, here), 96, 1)
        minus1 = pltpu.roll(jnp.where(lane >= 96, west, here), 32, 1)
        two = pltpu.roll(jnp.where(lane < 64, east - here, here - west), 64, 1)
        plus3 = pltpu.roll(jnp.where(lane < 96, east, here), 32, 1)
        minus3 = pltpu.roll(jnp.where(lane >= 32, west, here), 96, 1)
        lon = 45.0 * (plus1 - minus1) - 9.0 * two + (plus3 - minus3)
        upper = jnp.where(not_last, pltpu.roll(here, LANES - 1, 1), 0.0)
        lower = jnp.where(not_first, pltpu.roll(here, 1, 1), 0.0)
        return here, lat, lon, upper - lower, up1 + down1, plus1 + minus1

    def group_rates(x, g, h, store):
        r = pl.multiple_of(TOP + 8 * h, 8)
        begin = pl.multiple_of((g - 1) * LANES, LANES)
        inv_lon, inv_sq = metric[h, 0], metric[h, 1]
        centre = 2.0 + 2.0 * inv_sq
        u = x[1, g, pl.ds(r, 8), :] * inv_lon
        v = x[2, g, pl.ds(r, 8), :]
        w = x[3, g, pl.ds(r, 8), :] * 0.5
        rho = x[0, g, pl.ds(r, 8), :]
        nu = visc[0, pl.ds(pl.multiple_of(8 * h, 8), 8), pl.ds(begin, LANES)]

        def plain(f):
            here, lat, lon, lev, rows_sum, cols_sum = derivatives(x, f, g, r)
            lap = rows_sum + cols_sum * inv_sq - centre * here
            return here, lat, lon, lev, nu * lap - (u * lon + v * lat + w * lev)

        e, e_lat, e_lon, e_lev, e_rate = plain(4)
        here, _, lon, _, rate = plain(1)
        div = lon * inv_lon
        store(1, g, h, begin, here, rate - KAPPA_PRESS * (e_lon * inv_lon))
        here, lat, _, _, rate = plain(2)
        div = div + lat
        store(2, g, h, begin, here, rate - KAPPA_PRESS * e_lat)
        here, _, _, lev, rate = plain(3)
        div = div + 0.5 * lev
        store(3, g, h, begin, here, rate - (0.5 * KAPPA_PRESS) * e_lev - rho)
        here, _, _, _, rate = plain(0)
        store(0, g, h, begin, here, rate - div)
        store(4, g, h, begin, e, e_rate - GAMMA_HEAT * div)

    def correct(s, x, h, add):
        r = pl.multiple_of(TOP + 8 * h, 8)
        sign = jnp.where(h == 0, -1.0, 1.0)

        def step(k, carry):
            for one in range(2):
                g = 1 + 2 * k + one
                begin = pl.multiple_of((g - 1) * LANES, LANES)
                v = x[2, g, pl.ds(r, 8), :]
                nu = visc[0, pl.ds(pl.multiple_of(8 * h, 8), 8), pl.ds(begin, LANES)]

                def share(f):
                    near, middle, far = (
                        hz[s, h, f, g - 1, pl.ds(jnp.where(h == 0, 8 - o, o), 8), :]
                        for o in (1, 2, 3)
                    )
                    lat = sign * (0.75 * near - 0.15 * middle + (1.0 / 60.0) * far)
                    return lat, nu * near - v * lat

                e_lat, e_rate = share(4)
                v_lat, v_rate = share(2)
                add(2, g, h, begin, v_rate - KAPPA_PRESS * e_lat)
                add(4, g, h, begin, e_rate - GAMMA_HEAT * v_lat)
                add(0, g, h, begin, share(0)[1] - v_lat)
                add(1, g, h, begin, share(1)[1])
                add(3, g, h, begin, share(3)[1])
            return carry

        lax.fori_loop(0, GROUPS // 2, step, 0)

    def section(s, x, store, add):
        def block(i, carry):
            @pl.when(i == 1)
            def _():
                if s == 0:
                    pl.semaphore_wait(north_ready, 1)
                rim_copies(s, (1,))[0].start()
                wait_cols(s, x)

            def step(k, inside):
                for one in range(2):
                    g = jnp.where(i == 0, 2 + 2 * (k // 2) + one, 1 + (GROUPS - 1) * one)
                    group_rates(x, g, k % 2, store)
                return inside

            lax.fori_loop(0, jnp.where(i == 0, GROUPS - 2, 2), step, 0)
            return carry

        lax.fori_loop(0, 2, block, 0)

        def side(i, carry):
            h = jnp.where(low_a, 1 - i, i)
            wait_rows(s, h)
            correct(s, x, h, add)
            return carry

        lax.fori_loop(0, 2, side, 0)

    def store_first(f, g, h, begin, here, rate):
        x2[f, g, pl.ds(pl.multiple_of(TOP + 8 * h, 8), 8), :] = here + TIME_STEP * rate

    def store_second(f, g, h, begin, here, rate):
        before = x1[f, g, pl.ds(pl.multiple_of(TOP + 8 * h, 8), 8), :]
        out[0, f, pl.ds(pl.multiple_of(8 * h, 8), 8), pl.ds(begin, LANES)] = 0.5 * (
            before + here + TIME_STEP * rate
        )

    def add_first(f, g, h, begin, rate):
        x2[f, g, pl.ds(pl.multiple_of(TOP + 8 * h, 8), 8), :] += TIME_STEP * rate

    def add_second(f, g, h, begin, rate):
        out[0, f, pl.ds(pl.multiple_of(8 * h, 8), 8), pl.ds(begin, LANES)] += (
            0.5 * TIME_STEP * rate
        )

    section(0, x1, store_first, add_first)
    export(1, x2)
    for copy in rim_copies(1, (0, 3, 2)):
        copy.start()
    for h in range(2):
        send_half(1, x2, h)
    section(1, x2, store_second, add_second)

    for s, x in enumerate((x1, x2)):
        for copy in rim_copies(s):
            copy.wait_send()
        for h in range(2):
            for there, copy in [row_copy(s, x, h)] + col_copies(s, x, h):

                @pl.when(there)
                def _():
                    copy.wait_send()


def on_device(*operands):
    n_lat = lax.axis_size("lat")
    n_lon = lax.axis_size("lon")
    operands = list(operands)
    operands[2] = operands[2].reshape(LAT_BLOCK, 1, LANES)
    operands[3] = operands[3].reshape(LON_BLOCK, 1, LANES)
    operands = [pltpu.with_memory_space_constraint(x, pltpu.HBM) for x in operands]

    def body(*refs):
        kernel(n_lat, n_lon, *refs)

    def vmem(*shape):
        return pltpu.VMEM(shape, jnp.float32)

    return pl.pallas_call(
        body,
        out_shape=jax.ShapeDtypeStruct(operands[0].shape, jnp.float32),
        in_specs=[pl.BlockSpec(memory_space=pltpu.HBM)] * 10,
        out_specs=pl.BlockSpec(memory_space=pltpu.VMEM),
        scratch_shapes=[
            vmem(FIELDS, GROUPS + 2, 32, LANES),
            vmem(FIELDS, GROUPS + 2, 32, LANES),
            vmem(2, 2, FIELDS, GROUPS, 16, LANES),
            vmem(1, CLAT, GROUPS * LANES),
            vmem(LAT_BLOCK, 1, LANES),
            vmem(LON_BLOCK, 1, LANES),
            pltpu.SMEM((1, 1, 1, LAT_BLOCK), jnp.float32),
            pltpu.SMEM((1, 1, 1, LON_BLOCK), jnp.float32),
            pltpu.SMEM((1, 1, 1, 2), jnp.int32),
            pltpu.SMEM((1, 1, 1, 2), jnp.int32),
            pltpu.VMEM((2, 1, n_lat), jnp.int32),
            pltpu.VMEM((2, 1, n_lon), jnp.int32),
            vmem(32, 2 * LANES),
            pltpu.VMEM((2, LANES, GROUPS * CLAT), jnp.bfloat16),
            vmem(2, 2, 8, LANES),
            vmem(2, BLOCK_ROWS, LANES),
            vmem(2, 2, WIDE_ROWS, LANES),
            vmem(2 * n_lat * BLOCK_ROWS, LANES),
            vmem(2 * n_lon * WIDE_ROWS, LANES),
            pltpu.SemaphoreType.DMA((10,)),
            pltpu.SemaphoreType.DMA((2, 3, 2)),
            pltpu.SemaphoreType.DMA((2, 3, 2)),
            pltpu.SemaphoreType.DMA((2, 4)),
            pltpu.SemaphoreType.DMA((2, 2)),
            pltpu.SemaphoreType.REGULAR,
        ],
        compiler_params=pltpu.CompilerParams(
            collective_id=0, has_side_effects=True, vmem_limit_bytes=40 * 1024 * 1024
        ),
    )(*operands)


def solution(mesh):
    in_specs = (
        P("yy", None, "lat", "lon"),
        P("yy", "lat", "lon"),
        P("yy", "lat", "lon", None, None),
        P("yy", "lat", "lon", None, None),
        P("yy", "lat", "lon", None),
        P("yy", "lat", "lon", None),
        P("yy", "lat", "lon", None),
        P("yy", "lat", "lon", None),
        P(None, "lon", None),
        P(None, "lat", None),
    )
    out_specs = P("yy", None, "lat", "lon")
    return jax.shard_map(
        on_device, mesh=mesh, in_specs=in_specs, out_specs=out_specs, check_vma=False
    )
```
